128 devices in a mesh: front: 32 (over z, y, x_hi), row: 2 (over x_lo), col: 2 (over core).
Axes of the slice: x: 4 (x_hi: 2, x_lo: 2; x = x_hi * 2 + x_lo), y: 4, z: 4, core: 2. Of those that a mesh axis runs over, the one named last changes fastest.
Arguments:
- child_rows: float32 [32768, 8192], P(('front', 'row'), 'col'), may hold values from -20 to 20
- row_list: int32 [32768], P(('front', 'row')), may hold values from 0 to 32767, as said below
- orig_rows: float32 [24576, 8192], P(('front', 'row'), 'col'), may hold values from -20 to 20
- tile_mask: int32 [768], P(('front', 'row')), may hold values from 0 to 1, as said below
Outputs:
- factor_rows: float32 [32, 4, 256, 8192], P('front', None, 'row', 'col')
The draws below stay inside these ranges and needn't reach their ends.
Inputs may be any that keep to these rules, and one draw needn't show every extreme that they name: `row_list`: a permutation of all parent rows; of the 512 child rows held by one device, at most 16 have parent rows in any one aligned block of 512 parent rows, and in every draw some device sends exactly 16 rows to some block. `tile_mask`: where an entry is 0, the first 256 columns of that tile of orig_rows are zero.
All inputs are finite; a program needn't handle non-finite values.
Results may differ from the reference program's by a relative error of at most 0.00021.
Values sent between devices are 32-bit elements; how exact they have to be, the bound alone decides.
No kernel may reach another device: no remote copies, remote signals or barrier semaphores. Data moves between devices by JAX's collectives and lax.ppermute only.
A program may use at most 256 MiB of HBM per device.

```python
import jax
import jax.numpy as jnp
from jax import lax

NP = 8192
PANEL = 256
PANELS = 4
TILE = 32
FRONTS = 32
NPIV = 1024
PR = 1024
ROWS_DEV = 512
ORIG = 768
N_FRONT = 32
N_ROW = 2


def column_spread(key):
    return jax.random.uniform(jax.random.fold_in(key, 101), (NP,), jnp.float32, -1.0, 1.0)


def orig_leads(key):
    raw_leads = jax.random.randint(jax.random.fold_in(key, 202), (FRONTS, ORIG), 0, NPIV)
    return jnp.sort(raw_leads, axis=1)


def column_factor(spread):
    column_index = jnp.arange(NP)
    return jnp.where(column_index < NPIV, jnp.exp(0.35 * spread) * (PR + ORIG) ** (-0.5), jnp.exp(1.15 * spread))


def draw_child_rows(key, part):
    spread = column_spread(key)
    key = jax.random.fold_in(key, 1)
    entries = jnp.clip(jax.random.normal(key, (FRONTS * PR, NP), jnp.float32), -6.0, 6.0)
    return entries * column_factor(spread)[None, :]


def draw_orig_rows(key, part):
    spread = column_spread(key)
    lead_cols = orig_leads(key).reshape(-1)
    key = jax.random.fold_in(key, 2)
    entries = jnp.clip(jax.random.normal(key, (FRONTS * ORIG, NP), jnp.float32), -6.0, 6.0)
    live_part = (jnp.arange(NP)[None, :] >= lead_cols[:, None]).astype(jnp.float32)
    return entries * column_factor(spread)[None, :] * live_part


def draw_tile_mask(key, part):
    lead_cols = orig_leads(key)
    return (lead_cols[:, ::TILE] < PANEL).astype(jnp.int32).reshape(-1)


def draw_row_list(key, part):
    key = jax.random.fold_in(key, 3)
    groups = N_FRONT * N_ROW
    mean_count = ROWS_DEV // groups
    small_step = mean_count // 2
    large_step = mean_count - small_step
    subkeys = jax.random.split(key, 5)
    first_order = jax.random.permutation(subkeys[0], groups)
    second_order = jax.random.permutation(subkeys[1], groups)
    offset = jax.random.randint(subkeys[2], (), 0, groups // 2)
    third_order = (first_order + offset) % groups
    first_sign = jnp.where((first_order[:, None] + second_order[None, :]) % groups < groups // 2, 1, -1)
    second_sign = jnp.where((third_order[:, None] + second_order[None, :]) % groups < groups // 2, 1, -1)
    counts = mean_count + large_step * first_sign + small_step * second_sign
    starts = jnp.cumsum(counts, axis=1) - counts
    arrive_base = jnp.cumsum(counts, axis=0) - counts
    targets = jax.vmap(lambda row_counts: jnp.repeat(jnp.arange(groups), row_counts, total_repeat_length=ROWS_DEV))(counts)
    order_in = jnp.arange(ROWS_DEV)[None, :] - jnp.take_along_axis(starts, targets, axis=1)
    arrival = jnp.take_along_axis(arrive_base, targets, axis=1) + order_in
    slot_orders = jax.vmap(lambda split_key: jax.random.permutation(split_key, ROWS_DEV))(jax.random.split(subkeys[3], groups))
    slot_index = slot_orders[targets, arrival]
    parent_row = targets * ROWS_DEV + slot_index
    shuffles = jax.vmap(lambda split_key: jax.random.permutation(split_key, ROWS_DEV))(jax.random.split(subkeys[4], groups))
    return jnp.take_along_axis(parent_row, shuffles, axis=1).reshape(-1).astype(jnp.int32)


def setup_inputs(seed: int = 0) -> dict:
    keys = jax.random.split(jax.random.key(seed), 5)
    return {
        "child_rows": draw_child_rows(jax.random.fold_in(keys[4], 71), 0),
        "row_list": draw_row_list(jax.random.fold_in(keys[4], 71), 0),
        "orig_rows": draw_orig_rows(jax.random.fold_in(keys[4], 71), 0),
        "tile_mask": draw_tile_mask(jax.random.fold_in(keys[4], 71), 0),
    }


def reference(child_rows, row_list, orig_rows, tile_mask):
    placed = jnp.zeros_like(child_rows).at[row_list].set(child_rows).reshape(FRONTS, PR, NP)
    tile_keep = jnp.repeat(tile_mask, TILE).astype(jnp.float32).reshape(FRONTS, ORIG, 1)
    first_panel = (jnp.arange(NP) < PANEL).astype(jnp.float32)
    masked = orig_rows.reshape(FRONTS, ORIG, NP) * (1.0 - (1.0 - tile_keep) * first_panel)
    results = []
    for front_index in range(FRONTS):
        front_rows = jnp.concatenate([placed[front_index], masked[front_index]], axis=0)
        gram_front = jnp.dot(front_rows[:, :NPIV].T, front_rows, precision=lax.Precision.HIGHEST)
        lower_factor = jnp.linalg.cholesky(gram_front[:, :NPIV])
        factor_rows = jax.scipy.linalg.solve_triangular(lower_factor, gram_front, lower=True)
        results.append(factor_rows.reshape(PANELS, PANEL, NP))
    return jnp.stack(results)
```

```python
import functools

import jax
import jax.numpy as jnp
from jax import lax
from jax.experimental import pallas as pl
from jax.experimental.pallas import tpu as pltpu
from jax.sharding import Mesh, PartitionSpec as P

PANEL = 256
PANELS = 4
TILE = 32
NPIV = PANEL * PANELS
FRONTS = 32
SLOTS = 32
FRONT_CHILD = 1024
HALF = PANEL // 2
BASE = 8
LEAF = 128

CHIPS = ("z", "y", "h", "l")
NEAR = [[zy * 4 + x for zy in range(16) for x in pair] for pair in ((0, 3), (1, 2))]
SWAP = [(0, 1), (1, 0)]
CHUNKS = ((0, 1024), (1024, 1024), (2048, 1024), (3072, 1024))
CORE_BLOCKS = (
    ((0, 0), (0, 1), (0, 2), (0, 3), (1, 1)),
    ((1, 2), (1, 3), (2, 2), (2, 3), (3, 3)),
)
BLOCK_AT = {pair: at for at, pair in enumerate(CORE_BLOCKS[0] + CORE_BLOCKS[1])}

F32 = jnp.float32
BF16 = jnp.bfloat16
EXACT = lax.Precision.HIGHEST
VMEM_LIMIT = 48 * 1024 * 1024
NN = (((1,), (0,)), ((), ()))
NT = (((1,), (1,)), ((), ()))
TN = (((0,), (0,)), ((), ()))


def cost(flops, nbytes):
    return pl.CostEstimate(flops=int(flops), bytes_accessed=int(nbytes), transcendentals=0)


def split_two(value):
    high = value.astype(BF16)
    return high, (value - high.astype(F32)).astype(BF16)


def dot_split(left, right, dims=NN):
    out = lax.dot_general(left[0], right[0], dims, preferred_element_type=F32)
    out += lax.dot_general(left[0], right[1], dims, preferred_element_type=F32)
    return out + lax.dot_general(left[1], right[0], dims, preferred_element_type=F32)


def dot_exact(left, right, dims=NN):
    return lax.dot_general(left, right, dims, precision=EXACT, preferred_element_type=F32)


def send_kernel(list_ref, child_ref, out_ref, pick_ref):
    @pl.when(pl.program_id(0) == 0)
    def _():
        front = lax.shift_right_logical(list_ref[...], 10)
        rows = front.shape[1]
        hit = lax.broadcasted_iota(jnp.int32, (FRONTS, rows), 0) == front
        order = lax.broadcasted_iota(jnp.int32, (rows, rows), 0) <= lax.broadcasted_iota(
            jnp.int32, (rows, rows), 1
        )
        hit_one = jnp.where(hit, 1.0, 0.0)
        count = jnp.dot(
            hit_one.astype(BF16),
            jnp.where(order, 1.0, 0.0).astype(BF16),
            preferred_element_type=F32,
        )
        rank = jnp.sum(hit_one * count, axis=0, keepdims=True) - 1.0
        slot = front * SLOTS + rank.astype(jnp.int32)
        places = lax.broadcasted_iota(jnp.int32, (FRONTS * SLOTS, rows), 0)
        pick_ref[...] = jnp.where(places == slot, 1.0, 0.0).astype(BF16)

    value = child_ref[...]
    pick = pick_ref[...]
    high = value.astype(BF16)
    rest = value - high.astype(F32)
    middle = rest.astype(BF16)
    low = (rest - middle.astype(F32)).astype(BF16)
    out = jnp.dot(pick, high, preferred_element_type=F32)
    out += jnp.dot(pick, middle, preferred_element_type=F32)
    out_ref[...] = out + jnp.dot(pick, low, preferred_element_type=F32)


def send_rows(list_row, child_rows, first, width):
    rows = child_rows.shape[0]
    block = min(width, 512)
    return pl.pallas_call(
        send_kernel,
        grid=(width // block,),
        in_specs=[
            pl.BlockSpec((1, rows), lambda i: (0, 0)),
            pl.BlockSpec((rows, block), lambda i: (0, first // block + i)),
        ],
        out_specs=pl.BlockSpec((FRONTS * SLOTS, block), lambda i: (0, i)),
        out_shape=jax.ShapeDtypeStruct((FRONTS * SLOTS, width), F32),
        scratch_shapes=[pltpu.VMEM((FRONTS * SLOTS, rows), BF16)],
        compiler_params=pltpu.CompilerParams(vmem_limit_bytes=VMEM_LIMIT),
        cost_estimate=cost(6 * FRONTS * SLOTS * rows * width, 12 * rows * width),
        name="send_rows",
    )(list_row, child_rows)


def pivot_kernel(core_ref, own_ref, got_ref, orig_ref, orig_got_ref, keep_ref, high_ref, low_ref):
    is_first = core_ref[0] == 0
    child = jnp.where(is_first, own_ref[...], got_ref[...]).T
    orig = jnp.where(is_first, orig_ref[...], orig_got_ref[...])
    keep = jnp.where(pl.program_id(0) == 0, keep_ref[...], 1.0)
    orig = (orig * keep).T
    slots = child.shape[1]
    child_high, child_low = split_two(child)
    orig_high, orig_low = split_two(orig)
    high_ref[:, :slots] = child_high
    low_ref[:, :slots] = child_low
    high_ref[:, slots:] = orig_high
    low_ref[:, slots:] = orig_low


def pivot_columns(core, own, got, orig_rows, orig_got, keep):
    slots, orig = own.shape[0], orig_rows.shape[0]
    rows = slots + orig
    return pl.pallas_call(
        pivot_kernel,
        grid=(PANELS,),
        in_specs=[
            pl.BlockSpec(memory_space=pltpu.SMEM),
            pl.BlockSpec((slots, PANEL), lambda i: (0, i)),
            pl.BlockSpec((slots, PANEL), lambda i: (0, i)),
            pl.BlockSpec((orig, PANEL), lambda i: (0, i)),
            pl.BlockSpec((orig, PANEL), lambda i: (0, i)),
            pl.BlockSpec((orig, 1), lambda i: (0, 0)),
        ],
        out_specs=[pl.BlockSpec((PANEL, rows), lambda i: (i, 0))] * 2,
        out_shape=[jax.ShapeDtypeStruct((NPIV, rows), BF16)] * 2,
        compiler_params=pltpu.CompilerParams(vmem_limit_bytes=VMEM_LIMIT),
        cost_estimate=cost(rows * NPIV * 8, rows * NPIV * 12),
        name="pivot_columns",
    )(core, own, got, orig_rows, orig_got, keep)


def gram_kernel(left_at, right_at, lh_ref, ll_ref, rh_ref, rl_ref, out_ref):
    out_ref[0] = dot_split((lh_ref[...], ll_ref[...]), (rh_ref[...], rl_ref[...]), NT)


def gram_blocks(left_at, right_at, high, low):
    rows = high.shape[1]
    count = len(CORE_BLOCKS[0])
    left = pl.BlockSpec((PANEL, rows), lambda s, a, b: (a[s], 0))
    right = pl.BlockSpec((PANEL, rows), lambda s, a, b: (b[s], 0))
    return pl.pallas_call(
        gram_kernel,
        grid_spec=pltpu.PrefetchScalarGridSpec(
            num_scalar_prefetch=2,
            grid=(count,),
            in_specs=[left, left, right, right],
            out_specs=pl.BlockSpec((1, PANEL, PANEL), lambda s, a, b: (s, 0, 0)),
        ),
        out_shape=jax.ShapeDtypeStruct((count, PANEL, PANEL), F32),
        compiler_params=pltpu.CompilerParams(vmem_limit_bytes=VMEM_LIMIT),
        cost_estimate=cost(6 * count * PANEL * PANEL * rows, 8 * count * PANEL * rows),
        name="gram_blocks",
    )(left_at, right_at, high, low, high, low)


def factor_leaf(work):
    sub = lax.broadcasted_iota(jnp.int32, (BASE, 2 * LEAF), 0)
    for step in range(LEAF // BASE):
        top = step * BASE
        rows = work[top : top + BASE, :]
        shape = (BASE, 2 * LEAF)
        entry = [
            [
                jnp.broadcast_to(rows[j : j + 1, top + i : top + i + 1], shape)
                for j in range(i + 1)
            ]
            for i in range(BASE)
        ]
        inv_diag = []
        for j in range(BASE):
            inv_diag.append(lax.rsqrt(entry[j][j]))
            for i in range(j + 1, BASE):
                entry[i][j] = entry[i][j] * inv_diag[j]
            for i in range(j + 1, BASE):
                for k in range(j + 1, i + 1):
                    entry[i][k] = entry[i][k] - entry[i][j] * entry[k][j]
        inverse = [[None] * BASE for _ in range(BASE)]
        for i in range(BASE):
            inverse[i][i] = inv_diag[i]
            for j in range(i):
                total = entry[i][j] * inverse[j][j]
                for k in range(j + 1, i):
                    total = total + entry[i][k] * inverse[k][j]
                inverse[i][j] = -(total * inv_diag[i])
        done = None
        for j in range(BASE):
            column = inverse[j][j]
            for i in range(j + 1, BASE):
                column = jnp.where(sub == i, inverse[i][j], column)
            column = jnp.where(sub < j, 0.0, column)
            term = column * jnp.broadcast_to(rows[j : j + 1, :], shape)
            done = term if done is None else done + term
        work[top : top + BASE, :] = done
        below = top + BASE
        if below < LEAF:
            change = dot_exact(done[:, :LEAF], done, TN)
            work[below:, :] = work[below:, :] - change[below:, :]


def panel_kernel(panel, *refs):
    gram_ref, high_ref, low_ref = refs[:3]
    before = refs[3 : 3 + 3 * panel]
    row_ref, qh_ref, ql_ref = refs[3 + 3 * panel : 6 + 3 * panel]
    rest_ref, work, inv_ref = refs[6 + 3 * panel :]
    first = panel * PANEL
    count = PANELS - panel
    for j in range(count):
        rest_ref[:, j * PANEL : (j + 1) * PANEL] = gram_ref[BLOCK_AT[(panel, panel + j)]]
    span = count * PANEL
    pivots = (high_ref[...].astype(F32)) + (low_ref[...].astype(F32))
    for k in range(panel):
        old_ref, old_high, old_low = before[3 * k : 3 * k + 3]
        tie = old_ref[:, first : first + PANEL].T
        rest_ref[:, :span] = rest_ref[:, :span] - dot_exact(tie, old_ref[:, first:])
        pivots -= dot_split(split_two(tie), (old_high[...], old_low[...]))
    eye = jnp.where(
        lax.broadcasted_iota(jnp.int32, (LEAF, LEAF), 0)
        == lax.broadcasted_iota(jnp.int32, (LEAF, LEAF), 1),
        1.0,
        0.0,
    )
    work[:, :LEAF] = rest_ref[:LEAF, :LEAF]
    work[:, LEAF:] = eye
    factor_leaf(work)
    inv_first = work[:, LEAF:]
    upper = dot_exact(inv_first, rest_ref[:LEAF, LEAF:PANEL])
    work[:, :LEAF] = rest_ref[LEAF:PANEL, LEAF:PANEL] - dot_exact(upper, upper, TN)
    work[:, LEAF:] = eye
    inv_ref[:LEAF, :LEAF] = inv_first
    inv_ref[:LEAF, LEAF:] = jnp.zeros((LEAF, LEAF), F32)
    factor_leaf(work)
    inv_second = work[:, LEAF:]
    inv_ref[LEAF:, LEAF:] = inv_second
    inv_ref[LEAF:, :LEAF] = -dot_exact(inv_second, dot_exact(upper, inv_first, TN))
    inverse = inv_ref[...]
    if first:
        row_ref[:, :first] = jnp.zeros((PANEL, first), F32)
    row_ref[:, first:] = dot_exact(inverse, rest_ref[:, :span])
    qh_ref[...], ql_ref[...] = split_two(dot_split(split_two(inverse), split_two(pivots)))


def factor_panel(panel, gram, high, low, before):
    rows = high.shape[1]
    whole = pl.BlockSpec(memory_space=pltpu.VMEM)
    mine = pl.BlockSpec((PANEL, rows), lambda i: (panel, 0))
    flat = [value for triple in before for value in triple]
    full = lambda shape: pl.BlockSpec(shape, lambda i: (0,) * len(shape))
    return pl.pallas_call(
        functools.partial(panel_kernel, panel),
        grid=(1,),
        in_specs=[full(gram.shape), mine, mine] + [full(value.shape) for value in flat],
        out_specs=[full((PANEL, NPIV)), full((PANEL, rows)), full((PANEL, rows))],
        out_shape=[
            jax.ShapeDtypeStruct((PANEL, NPIV), F32),
            jax.ShapeDtypeStruct((PANEL, rows), BF16),
            jax.ShapeDtypeStruct((PANEL, rows), BF16),
        ],
        scratch_shapes=[
            pltpu.VMEM((PANEL, NPIV), F32),
            pltpu.VMEM((LEAF, 2 * LEAF), F32),
            pltpu.VMEM((PANEL, PANEL), F32),
        ],
        compiler_params=pltpu.CompilerParams(vmem_limit_bytes=VMEM_LIMIT),
        cost_estimate=cost(2e10, 8e6),
        name=f"factor_panel_{panel}",
    )(gram, high, low, *flat)


def project_kernel(count, side_ref, child_ref, orig_ref, *refs):
    q_refs, (keep_ref, send_ref, total) = refs[: 2 * count], refs[2 * count :]
    slots = child_ref.shape[0]
    child = split_two(child_ref[...])
    orig = split_two(orig_ref[...])
    high = jnp.concatenate([ref[...] for ref in q_refs[0::2]], axis=0)
    low = jnp.concatenate([ref[...] for ref in q_refs[1::2]], axis=0)
    total[...] = dot_split((high[:, :slots], low[:, :slots]), child) + dot_split(
        (high[:, slots:], low[:, slots:]), orig
    )
    side = side_ref[0]
    for i in range(count):
        keep_ref[i] = total[pl.ds(i * PANEL + side * HALF, HALF), :]
        send_ref[i] = total[pl.ds(i * PANEL + (1 - side) * HALF, HALF), :]


def project(side, child, orig_rows, first, bases):
    slots, width = child.shape
    orig = orig_rows.shape[0]
    count = len(bases)
    block = min(width, 512)
    flat = [value for pair in bases for value in pair]
    out = pl.BlockSpec((count, HALF, block), lambda i: (0, 0, i))
    return pl.pallas_call(
        functools.partial(project_kernel, count),
        grid=(width // block,),
        in_specs=[
            pl.BlockSpec(memory_space=pltpu.SMEM),
            pl.BlockSpec((slots, block), lambda i: (0, i)),
            pl.BlockSpec((orig, block), lambda i: (0, first // block + i)),
        ]
        + [pl.BlockSpec(value.shape, lambda i: (0, 0)) for value in flat],
        out_specs=[out, out],
        out_shape=[jax.ShapeDtypeStruct((count, HALF, width), F32)] * 2,
        scratch_shapes=[pltpu.VMEM((count * PANEL, block), F32)],
        compiler_params=pltpu.CompilerParams(vmem_limit_bytes=VMEM_LIMIT),
        cost_estimate=cost(
            6 * count * PANEL * (slots + orig) * width, 4 * (slots + orig + count * PANEL) * width
        ),
        name="project",
    )(side, child, orig_rows, *flat)


def body(child_rows, row_list, orig_rows, tile_mask):
    core = lax.axis_index("c")
    side = lax.axis_index("l")
    core_one = core.astype(jnp.int32).reshape(1)
    side_one = side.astype(jnp.int32).reshape(1)
    list_row = row_list.reshape(1, -1)

    got_rows = []
    for first, width in CHUNKS:
        sent = send_rows(list_row, child_rows, first, width)
        got = lax.all_to_all(
            sent.reshape(FRONTS, SLOTS, width),
            CHIPS,
            0,
            0,
            axis_index_groups=NEAR,
            tiled=True,
        )
        got_rows.append(got.reshape(FRONTS * SLOTS, width))

    orig_first = lax.ppermute(orig_rows[:, :NPIV], "c", [(0, 1)])
    child_first = lax.ppermute(got_rows[0], "c", [(0, 1)])
    keep = jnp.repeat(tile_mask, TILE).astype(F32)[:, None]
    high, low = pivot_columns(core_one, got_rows[0], child_first, orig_rows, orig_first, keep)
    tables = jnp.array(CORE_BLOCKS, jnp.int32)[core]
    part = gram_blocks(tables[:, 0], tables[:, 1], high, low)
    part = part + lax.ppermute(part, "l", SWAP)
    other = lax.ppermute(part, "c", SWAP)
    gram = jnp.where(
        core == 0, jnp.concatenate([part, other]), jnp.concatenate([other, part])
    )

    before = []
    for panel in range(PANELS):
        before.append(factor_panel(panel, gram, high, low, before))
    bases = [(q_high, q_low) for _, q_high, q_low in before]

    pieces = []
    for index, (first, width) in enumerate(CHUNKS):
        mine, theirs = project(side_one, got_rows[index], orig_rows, first, bases)
        if index == 0:
            total = mine + lax.ppermute(theirs, ("l", "c"), [(1, 3), (3, 1)])
            pivot_rows = jnp.stack([row for row, _, _ in before])
            pivot_rows = lax.dynamic_slice_in_dim(pivot_rows, side * HALF, HALF, 1)
            pieces.append(jnp.where(core == 0, pivot_rows, total))
        else:
            pieces.append(mine + lax.ppermute(theirs, "l", SWAP))
    return jnp.concatenate(pieces, axis=2)[None]


def solution(mesh):
    chips = Mesh(mesh.devices.reshape(4, 4, 2, 2, 2), CHIPS + ("c",))
    placed = (P(CHIPS, "c"), P(CHIPS), P(CHIPS, "c"), P(CHIPS))
    return jax.shard_map(
        body,
        mesh=chips,
        in_specs=placed,
        out_specs=P(("z", "y", "h"), None, "l", "c"),
        check_vma=False,
    )
```

```python
import functools

import jax
import jax.numpy as jnp
from jax import lax
from jax.experimental import pallas as pl
from jax.experimental.pallas import tpu as pltpu
from jax.sharding import Mesh, PartitionSpec as P

PANEL = 256
PANELS = 4
TILE = 32
NPIV = PANEL * PANELS
FRONTS = 32
SLOTS = 32
FRONT_CHILD = 1024
HALF = PANEL // 2
BASE = 8
LEAF = 128

CHIPS = ("z", "y", "h", "l")
NEAR = [[zy * 4 + x for zy in range(16) for x in pair] for pair in ((0, 3), (1, 2))]
SWAP = [(0, 1), (1, 0)]
CHUNKS = ((512, 1536), (2048, 1024), (3072, 512), (3584, 512))
SHARE = 512
ROUNDS = (
    (((0, 1), (0, 2)), ((0, 3), (1, 1))),
    (((1, 2), (1, 3), (3, 3)), ((2, 2), (2, 3), (0, 0))),
)

F32 = jnp.float32
BF16 = jnp.bfloat16
EXACT = lax.Precision.HIGHEST
VMEM_LIMIT = 60 * 1024 * 1024
NN = (((1,), (0,)), ((), ()))
NT = (((1,), (1,)), ((), ()))
TN = (((0,), (0,)), ((), ()))


def cost(micros):
    return pl.CostEstimate(
        flops=int(micros * 1.1e9), bytes_accessed=int(micros * 3.5e6), transcendentals=0
    )


def split_two(value):
    high = value.astype(BF16)
    return high, (value - high.astype(F32)).astype(BF16)


def dot_split(left, right, dims=NN):
    out = lax.dot_general(left[0], right[0], dims, preferred_element_type=F32)
    out += lax.dot_general(left[0], right[1], dims, preferred_element_type=F32)
    return out + lax.dot_general(left[1], right[0], dims, preferred_element_type=F32)


def dot_exact(left, right, dims=NN):
    return lax.dot_general(left, right, dims, precision=EXACT, preferred_element_type=F32)


def pick_kernel(list_ref, pick_ref):
    front = lax.shift_right_logical(list_ref[...], 10)
    rows = front.shape[1]
    hit = lax.broadcasted_iota(jnp.int32, (FRONTS, rows), 0) == front
    order = lax.broadcasted_iota(jnp.int32, (rows, rows), 0) <= lax.broadcasted_iota(
        jnp.int32, (rows, rows), 1
    )
    hit_one = jnp.where(hit, 1.0, 0.0)
    count = jnp.dot(
        hit_one.astype(BF16),
        jnp.where(order, 1.0, 0.0).astype(BF16),
        preferred_element_type=F32,
    )
    rank = jnp.sum(hit_one * count, axis=0, keepdims=True) - 1.0
    slot = front * SLOTS + rank.astype(jnp.int32)
    places = lax.broadcasted_iota(jnp.int32, (FRONTS * SLOTS, rows), 0)
    pick_ref[...] = jnp.where(places == slot, 1.0, 0.0).astype(BF16)


def pick_matrix(list_row):
    rows = list_row.shape[1]
    return pl.pallas_call(
        pick_kernel,
        out_shape=jax.ShapeDtypeStruct((FRONTS * SLOTS, rows), BF16),
        compiler_params=pltpu.CompilerParams(vmem_limit_bytes=VMEM_LIMIT),
        cost_estimate=cost(2),
        name="pick_matrix",
    )(list_row)


def place_rows(pick, value, out_ref):
    high = value.astype(BF16)
    rest = value - high.astype(F32)
    middle = rest.astype(BF16)
    low = (rest - middle.astype(F32)).astype(BF16)
    out = jnp.dot(pick, high, preferred_element_type=F32)
    out += jnp.dot(pick, middle, preferred_element_type=F32)
    out_ref[...] = out + jnp.dot(pick, low, preferred_element_type=F32)


def send_kernel(pick_ref, child_ref, out_ref):
    place_rows(pick_ref[...], child_ref[...], out_ref)


def send_share_kernel(own_ref, pick_ref, child_ref, got_ref, out_ref):
    use_got = jnp.logical_and(pl.program_id(0) < SHARE // got_ref.shape[1], own_ref[0] == 0)
    value = jnp.where(use_got, got_ref[...], child_ref[...])
    place_rows(pick_ref[...], value, out_ref)


def send_rows(pick, child_rows, first, width, use_own=None, got=None):
    rows = child_rows.shape[0]
    block = 256 if width == SHARE else 512
    specs = [
        pl.BlockSpec(pick.shape, lambda i: (0, 0)),
        pl.BlockSpec((rows, block), lambda i: (0, first // block + i)),
    ]
    values = [pick, child_rows]
    if got is not None:
        specs = [pl.BlockSpec(memory_space=pltpu.SMEM)] + specs
        last = SHARE // block - 1
        specs.append(pl.BlockSpec((rows, block), lambda i: (0, jnp.minimum(i, last))))
        values = [use_own] + values + [got]
    return pl.pallas_call(
        send_kernel if got is None else send_share_kernel,
        grid=(width // block,),
        in_specs=specs,
        out_specs=pl.BlockSpec((FRONTS * SLOTS, block), lambda i: (0, i)),
        out_shape=jax.ShapeDtypeStruct((FRONTS * SLOTS, width), F32),
        compiler_params=pltpu.CompilerParams(vmem_limit_bytes=VMEM_LIMIT),
        cost_estimate=cost(3 + width / 256),
        name="send_rows",
    )(*values)


def pivot_kernel(core_ref, own_ref, got_ref, orig_ref, orig_got_ref, keep_ref, high_ref, low_ref):
    step = pl.program_id(0)
    core = core_ref[0]
    child = jnp.where(step // 2 == core, own_ref[...], got_ref[...]).T
    orig = jnp.where(core == 0, orig_ref[...], orig_got_ref[...])
    keep = jnp.where(step == 0, keep_ref[...], 1.0)
    orig = (orig * keep).T
    slots = child.shape[1]
    child_high, child_low = split_two(child)
    orig_high, orig_low = split_two(orig)
    high_ref[:, :slots] = child_high
    low_ref[:, :slots] = child_low
    high_ref[:, slots:] = orig_high
    low_ref[:, slots:] = orig_low


def pivot_columns(core, own, got, orig_rows, orig_got, keep):
    slots, orig = own.shape[0], orig_rows.shape[0]
    rows = slots + orig
    return pl.pallas_call(
        pivot_kernel,
        grid=(PANELS,),
        in_specs=[
            pl.BlockSpec(memory_space=pltpu.SMEM),
            pl.BlockSpec((slots, PANEL), lambda i: (0, i % 2)),
            pl.BlockSpec((slots, PANEL), lambda i: (0, i % 2)),
            pl.BlockSpec((orig, PANEL), lambda i: (0, i)),
            pl.BlockSpec((orig, PANEL), lambda i: (0, i)),
            pl.BlockSpec((orig, 1), lambda i: (0, 0)),
        ],
        out_specs=[pl.BlockSpec((PANEL, rows), lambda i: (i, 0))] * 2,
        out_shape=[jax.ShapeDtypeStruct((NPIV, rows), BF16)] * 2,
        compiler_params=pltpu.CompilerParams(vmem_limit_bytes=VMEM_LIMIT),
        cost_estimate=cost(8),
        name="pivot_columns",
    )(core, own, got, orig_rows, orig_got, keep)


def gram_kernel(left_at, right_at, lh_ref, ll_ref, rh_ref, rl_ref, out_ref):
    out_ref[0] = dot_split((lh_ref[...], ll_ref[...]), (rh_ref[...], rl_ref[...]), NT)


def gram_blocks(left_at, right_at, high, low):
    rows = high.shape[1]
    count = left_at.shape[0]
    left = pl.BlockSpec((PANEL, rows), lambda s, a, b: (a[s], 0))
    right = pl.BlockSpec((PANEL, rows), lambda s, a, b: (b[s], 0))
    return pl.pallas_call(
        gram_kernel,
        grid_spec=pltpu.PrefetchScalarGridSpec(
            num_scalar_prefetch=2,
            grid=(count,),
            in_specs=[left, left, right, right],
            out_specs=pl.BlockSpec((1, PANEL, PANEL), lambda s, a, b: (s, 0, 0)),
        ),
        out_shape=jax.ShapeDtypeStruct((count, PANEL, PANEL), F32),
        compiler_params=pltpu.CompilerParams(vmem_limit_bytes=VMEM_LIMIT),
        cost_estimate=cost(2 + 1.5 * count),
        name="gram_blocks",
    )(left_at, right_at, high, low, high, low)


def split_three(value):
    high = value.astype(BF16).astype(F32)
    rest = value - high
    middle = rest.astype(BF16).astype(F32)
    return high, middle, rest - middle


def factor_leaf(square_ref, inv_ref, cols_ref):
    shape = (BASE, LEAF)
    sub = lax.broadcasted_iota(jnp.int32, shape, 0)
    lane = lax.broadcasted_iota(jnp.int32, shape, 1)
    for step in range(LEAF // BASE):
        top = step * BASE
        below = top + BASE
        rows = square_ref[top:below, :]
        unit = jnp.where(lane == sub + top, 1.0, 0.0)
        tail = unit if step == 0 else inv_ref[top:below, :]
        for j in range(BASE):
            cols_ref[BASE * j : BASE * j + BASE, :] = jnp.broadcast_to(
                rows[:, top + j : top + j + 1], shape
            )
        entry = [
            [
                jnp.broadcast_to(cols_ref[BASE * j + i : BASE * j + i + 1, :], shape)
                for j in range(i + 1)
            ]
            for i in range(BASE)
        ]
        inv_diag = []
        for j in range(BASE):
            inv_diag.append(lax.rsqrt(entry[j][j]))
            for i in range(j + 1, BASE):
                entry[i][j] = entry[i][j] * inv_diag[j]
            for i in range(j + 1, BASE):
                for k in range(j + 1, i + 1):
                    entry[i][k] = entry[i][k] - entry[i][j] * entry[k][j]
        inverse = [[None] * BASE for _ in range(BASE)]
        for i in range(BASE):
            inverse[i][i] = inv_diag[i]
            for j in range(i):
                total = entry[i][j] * inverse[j][j]
                for k in range(j + 1, i):
                    total = total + entry[i][k] * inverse[k][j]
                inverse[i][j] = -(total * inv_diag[i])
        done_rows, done_tail = None, None
        for j in range(BASE):
            column = inverse[j][j]
            for i in range(j + 1, BASE):
                column = jnp.where(sub == i, inverse[i][j], column)
            if j:
                column = jnp.where(sub < j, 0.0, column)
            row_term = column * jnp.broadcast_to(square_ref[top + j : top + j + 1, :], shape)
            tail_term = column * jnp.broadcast_to(tail[j : j + 1, :], shape)
            done_rows = row_term if done_rows is None else done_rows + row_term
            done_tail = tail_term if done_tail is None else done_tail + tail_term
        inv_ref[top:below, :] = done_tail
        if below < LEAF:
            rh, rm, rl = split_three(done_rows)
            th, tm, tl = split_three(done_tail)
            left = jnp.concatenate([rh, rh, rm, rh, rl, rm], axis=0).astype(BF16)
            right = jnp.concatenate([rh, rm, rh, rl, rh, rm], axis=0).astype(BF16)
            right_tail = jnp.concatenate([th, tm, th, tl, th, tm], axis=0).astype(BF16)
            change = lax.dot_general(
                left, jnp.concatenate([right, right_tail], axis=1), TN, preferred_element_type=F32
            )
            square_ref[below:, :] = square_ref[below:, :] - change[below:, :LEAF]
            if step == 0:
                later = jnp.where(
                    lax.broadcasted_iota(jnp.int32, (LEAF, LEAF), 0)
                    == lax.broadcasted_iota(jnp.int32, (LEAF, LEAF), 1),
                    1.0,
                    0.0,
                )
                inv_ref[below:, :] = later[below:, :] - change[below:, LEAF:]
            else:
                inv_ref[below:, :] = inv_ref[below:, :] - change[below:, LEAF:]


def gram_block(pair, is_first, own_ref, got_ref):
    for blocks in ROUNDS:
        for core, names in enumerate(blocks):
            if pair in names:
                at = names.index(pair)
                mine = is_first if core == 0 else jnp.logical_not(is_first)
                return jnp.where(mine, own_ref[at], got_ref[at])


def panel_kernel(panel, *refs):
    core_ref, high_ref, low_ref, own_ref, got_ref = refs[:5]
    refs = refs[5:]
    is_first = core_ref[0] == 0
    if panel == 0:
        rows, bases = [], []
        inv_out, diag_out, qh_ref, ql_ref, work, inv_ref, cols_ref = refs
        square = own_ref[...] + got_ref[...]
    else:
        rows = list(refs[: panel - 1])
        refs = refs[panel - 1 :]
        bases = refs[: 2 * panel]
        last_inv, last_diag = refs[2 * panel : 2 * panel + 2]
        inv_out, diag_out, qh_ref, ql_ref, row_out, work, inv_ref, cols_ref = refs[2 * panel + 2 :]
        last = panel - 1
        first = panel * PANEL
        behind = jnp.concatenate(
            [gram_block((last, j), is_first, own_ref, got_ref) for j in range(panel, PANELS)],
            axis=1,
        )
        for old in rows:
            tie = old[:, last * PANEL : first].T
            behind -= dot_exact(tie, old[:, first:])
        if last:
            row_out[:, : last * PANEL] = jnp.zeros((PANEL, last * PANEL), F32)
        row_out[:, last * PANEL : first] = last_diag[...]
        row_out[:, first:] = dot_exact(last_inv[...], behind)
        rows.append(row_out)
        square = gram_block((panel, panel), is_first, own_ref, got_ref)
    pivots = high_ref[...].astype(F32) + low_ref[...].astype(F32)
    for k, old in enumerate(rows):
        tie = old[:, panel * PANEL : (panel + 1) * PANEL].T
        square -= dot_exact(tie, tie, NT)
        pivots -= dot_split(split_two(tie), (bases[2 * k][...], bases[2 * k + 1][...]))
    work[...] = square[:LEAF, :LEAF]
    factor_leaf(work, inv_ref, cols_ref)
    inv_first = inv_ref[...]
    upper = dot_exact(inv_first, square[:LEAF, LEAF:])
    work[...] = square[LEAF:, LEAF:] - dot_exact(upper, upper, TN)
    inv_out[:LEAF, :LEAF] = inv_first
    inv_out[:LEAF, LEAF:] = jnp.zeros((LEAF, LEAF), F32)
    factor_leaf(work, inv_ref, cols_ref)
    inv_second = inv_ref[...]
    inv_out[LEAF:, LEAF:] = inv_second
    inv_out[LEAF:, :LEAF] = -dot_exact(inv_second, dot_exact(upper, inv_first, TN))
    inverse = inv_out[...]
    diag_out[...] = dot_exact(inverse, square)
    qh_ref[...], ql_ref[...] = split_two(dot_split(split_two(inverse), split_two(pivots)))


def factor_panel(panel, core, high, low, own, got, rows, bases, last):
    count = high.shape[1]
    mine = pl.BlockSpec((PANEL, count), lambda i: (panel, 0))
    flat = [*rows, *[value for pair in bases for value in pair], *last]
    full = lambda value: pl.BlockSpec(value.shape, lambda i: (0,) * len(value.shape))
    outs = [jax.ShapeDtypeStruct((PANEL, PANEL), F32)] * 2
    outs += [jax.ShapeDtypeStruct((PANEL, count), BF16)] * 2
    if panel:
        outs.append(jax.ShapeDtypeStruct((PANEL, NPIV), F32))
    return pl.pallas_call(
        functools.partial(panel_kernel, panel),
        grid=(1,),
        in_specs=[pl.BlockSpec(memory_space=pltpu.SMEM), mine, mine, full(own), full(got)]
        + [full(value) for value in flat],
        out_specs=[full(value) for value in outs],
        out_shape=outs,
        scratch_shapes=[pltpu.VMEM((LEAF, LEAF), F32)] * 2 + [pltpu.VMEM((BASE * BASE, LEAF), F32)],
        compiler_params=pltpu.CompilerParams(vmem_limit_bytes=VMEM_LIMIT),
        cost_estimate=cost(15),
        name=f"factor_panel_{panel}",
    )(core, high, low, own, got, *flat)


def project_kernel(count, shared, place_ref, child_ref, orig_ref, *refs):
    if shared:
        other_ref, refs = refs[0], refs[1:]
        use_other = jnp.logical_and(pl.program_id(0) == 0, place_ref[1] == 0)
        orig = jnp.where(use_other, other_ref[...], orig_ref[...])
    else:
        orig = orig_ref[...]
    q_refs, (keep_ref, send_ref, total) = refs[: 2 * count], refs[2 * count :]
    slots = child_ref.shape[0]
    child = split_two(child_ref[...])
    orig = split_two(orig)
    high = jnp.concatenate([ref[...] for ref in q_refs[0::2]], axis=0)
    low = jnp.concatenate([ref[...] for ref in q_refs[1::2]], axis=0)
    total[...] = dot_split((high[:, :slots], low[:, :slots]), child) + dot_split(
        (high[:, slots:], low[:, slots:]), orig
    )
    side = place_ref[0]
    for i in range(count):
        keep_ref[i] = total[pl.ds(i * PANEL + side * HALF, HALF), :]
        send_ref[i] = total[pl.ds(i * PANEL + (1 - side) * HALF, HALF), :]


def project(place, child, orig_rows, first, skip, width, bases, other, hides):
    slots = child.shape[0]
    orig = orig_rows.shape[0]
    count = len(bases)
    block = 512
    flat = [value for pair in bases for value in pair]
    specs = [pl.BlockSpec(value.shape, lambda i: (0, 0)) for value in flat]
    if other is not None:
        flat = [other] + flat
        specs = [pl.BlockSpec((orig, block), lambda i: (0, 0))] + specs
    out = pl.BlockSpec((count, HALF, block), lambda i: (0, 0, i))
    return pl.pallas_call(
        functools.partial(project_kernel, count, other is not None),
        grid=(width // block,),
        in_specs=[
            pl.BlockSpec(memory_space=pltpu.SMEM),
            pl.BlockSpec((slots, block), lambda i: (0, skip // block + i)),
            pl.BlockSpec((orig, block), lambda i: (0, (first + skip) // block + i)),
        ]
        + specs,
        out_specs=[out, out],
        out_shape=[jax.ShapeDtypeStruct((count, HALF, width), F32)] * 2,
        scratch_shapes=[pltpu.VMEM((count * PANEL, block), F32)],
        compiler_params=pltpu.CompilerParams(vmem_limit_bytes=VMEM_LIMIT),
        cost_estimate=cost(15 if hides else 0.5),
        name="project",
    )(place, child, orig_rows, *flat)


def combine_kernel(groups, core_ref, pivot_ref, extra_ref, other_ref, *refs):
    refs, out_ref = refs[:-1], refs[-1]
    panel = pl.program_id(0)
    is_first = core_ref[0] == 0
    out_ref[0, :, :SHARE] = jnp.where(is_first, pivot_ref[0, :, :SHARE], other_ref[0])
    out_ref[0, :, SHARE:NPIV] = jnp.where(is_first, pivot_ref[0, :, SHARE:], extra_ref[0])
    at = 0
    for base, width, first, count in groups:
        mine, got = refs[at : at + 2]
        at += 2

        @pl.when(jnp.logical_and(panel >= first, panel < first + count))
        def _():
            out_ref[0, :, base : base + width] = mine[0] + got[0]


def combine(core, pivot_rows, extra, other, parts, columns):
    groups, values, firsts = [], [pivot_rows, extra, other], [0, 0, 0]
    base = NPIV
    for pairs in parts:
        first = 0
        for mine, got in pairs:
            groups.append((base, mine.shape[2], first, mine.shape[0]))
            values += [mine, got]
            firsts += [first, first]
            first += mine.shape[0]
        base += pairs[0][0].shape[2]

    def spec(value, first):
        panels, half, width = value.shape
        return pl.BlockSpec(
            (1, half, width), lambda p: (jnp.clip(p - first, 0, panels - 1), 0, 0)
        )

    return pl.pallas_call(
        functools.partial(combine_kernel, groups),
        grid=(PANELS,),
        in_specs=[pl.BlockSpec(memory_space=pltpu.SMEM)]
        + [spec(value, first) for value, first in zip(values, firsts)],
        out_specs=pl.BlockSpec((1, HALF, columns), lambda p: (p, 0, 0)),
        out_shape=jax.ShapeDtypeStruct((PANELS, HALF, columns), F32),
        compiler_params=pltpu.CompilerParams(vmem_limit_bytes=VMEM_LIMIT),
        cost_estimate=cost(15),
        name="combine",
    )(core, *values)


def finish_kernel(mine_ref, got_ref, _, out_ref):
    out_ref[...] = mine_ref[...] + got_ref[...]


def finish(mine, got, result):
    panels, half, width = mine.shape
    last = result.shape[2] // width - 1
    part = pl.BlockSpec((panels // 2, half, width), lambda p: (p, 0, 0))
    return pl.pallas_call(
        finish_kernel,
        grid=(2,),
        in_specs=[part, part, pl.BlockSpec(memory_space=pl.ANY)],
        out_specs=pl.BlockSpec((panels // 2, half, width), lambda p: (p, 0, last)),
        out_shape=jax.ShapeDtypeStruct(result.shape, F32),
        input_output_aliases={2: 0},
        compiler_params=pltpu.CompilerParams(vmem_limit_bytes=VMEM_LIMIT),
        cost_estimate=cost(2),
        name="finish",
    )(mine, got, result)


def exchange(sent):
    width = sent.shape[1]
    got = lax.all_to_all(
        sent.reshape(FRONTS, SLOTS, width), CHIPS, 0, 0, axis_index_groups=NEAR, tiled=True
    )
    return got.reshape(FRONTS * SLOTS, width)


def body(child_rows, row_list, orig_rows, tile_mask):
    core = lax.axis_index("c")
    side = lax.axis_index("l")
    core_one = core.astype(jnp.int32).reshape(1)
    place = jnp.stack([side, core]).astype(jnp.int32)

    latest = [None]

    def then(value, *others):
        waits = [other for other in (latest[0], *others) if other is not None]
        return lax.optimization_barrier((value, *waits))[0] if waits else value

    def did(value):
        latest[0] = value
        return value

    def next_chunk(got, sent, *waits):
        got, sent, *_ = lax.optimization_barrier((got, sent, latest[0], *waits))
        latest[0] = got
        return got, exchange(sent)

    give = lax.dynamic_slice_in_dim(child_rows, (1 - core) * SHARE, SHARE, axis=1)
    take = lax.ppermute(give, "c", SWAP)
    pick = did(pick_matrix(row_list.reshape(1, -1)))
    sent_pivot = did(send_rows(then(pick), child_rows, 0, SHARE, 1 - core_one, take))
    got_pivot = exchange(sent_pivot)
    orig_got = lax.ppermute(then(orig_rows)[:, :NPIV], "c", SWAP)
    sents = [did(send_rows(then(pick), child_rows, *CHUNKS[0], core_one, take))]
    sents.append(did(send_rows(then(pick), child_rows, *CHUNKS[1])))
    sents.append(did(send_rows(then(pick), child_rows, *CHUNKS[2])))
    sents.append(did(send_rows(then(pick, orig_got), child_rows, *CHUNKS[3])))
    got_pivot, coming = next_chunk(got_pivot, sents[0])
    pivot_other = lax.ppermute(got_pivot, "c", SWAP)

    keep = jnp.repeat(tile_mask, TILE).astype(F32)[:, None]
    high, low = pivot_columns(core_one, then(got_pivot), pivot_other, orig_rows, orig_got, keep)
    did(high)
    zero = jnp.zeros((1,), jnp.int32)
    corner = did(gram_blocks(zero, zero, then(high), low))
    corner_got = lax.ppermute(corner, "l", SWAP)
    parts, sums = [], []

    def gram_round():
        table = jnp.array(ROUNDS[len(parts)], jnp.int32)[core]
        part = did(gram_blocks(table[:, 0], table[:, 1], then(high), low))
        parts.append((part, lax.ppermute(part, "l", SWAP)))

    def sum_round():
        part, got = parts[len(sums)]
        part = part + then(got)
        sums.append((part, lax.ppermute(part, "c", SWAP)))

    gram_round()
    rows, bases, last = [], [], []

    def panel_step(*waits):
        panel = len(bases)
        own, got = (corner[0], corner_got[0]) if panel == 0 else sums[min(panel - 1, 1)]
        out = factor_panel(panel, core_one, then(high, *waits), low, own, got, rows, bases, last)
        if panel:
            rows.append(out[4])
        bases.append(out[2:4])
        last[:] = out[:2]
        did(out[2])

    def rows_of(panels, child, index, *waits, skip=0, width=SHARE, other=None, hides=False):
        mine, theirs = project(
            place,
            then(child, *waits),
            orig_rows,
            CHUNKS[index][0],
            skip,
            width,
            [bases[p] for p in panels],
            other,
            hides,
        )
        did(theirs)
        return mine, lax.ppermute(theirs, "l", SWAP)

    every = (0, 1, 2, 3)
    panel_step()
    sum_round()
    gram_round()
    panel_step()
    sum_round()
    panel_step()
    here, coming = next_chunk(coming, sents[1])
    shared_early = rows_of((0, 1, 2), here, 0, other=orig_got)
    early = rows_of((0, 1, 2), here, 0, skip=SHARE, width=1024, hides=True)
    panel_step(shared_early[1])
    second_here, coming = next_chunk(coming, sents[2])
    late = rows_of((3,), here, 0, early[1], width=1536, other=orig_got)
    second = rows_of(every, second_here, 1, width=1024, hides=True)
    third_here, coming = next_chunk(coming, sents[3], late[1])
    third = rows_of(every, third_here, 2)
    mine, got = rows_of(every, coming, 3, second[1], hides=True)

    shared_late, late = [tuple(v[:, :, at] for v in late) for at in (slice(SHARE), slice(SHARE, None))]
    extra = jnp.concatenate([part[0] + part[1] for part in (shared_early, shared_late)])
    other_extra = lax.ppermute(extra, "c", [(0, 1)])
    pivot_rows = jnp.stack(rows + [jnp.pad(last[1], ((0, 0), (NPIV - PANEL, 0)))])
    pivot_rows = lax.dynamic_slice_in_dim(pivot_rows, side * HALF, HALF, 1)
    result = combine(
        core_one,
        then(pivot_rows),
        extra,
        other_extra,
        ([early, late], [second], [third]),
        child_rows.shape[1],
    )
    return finish(mine, got, result)[None]


def solution(mesh):
    chips = Mesh(mesh.devices.reshape(4, 4, 2, 2, 2), CHIPS + ("c",))
    placed = (P(CHIPS, "c"), P(CHIPS), P(CHIPS, "c"), P(CHIPS))
    return jax.shard_map(
        body,
        mesh=chips,
        in_specs=placed,
        out_specs=P(("z", "y", "h"), None, "l", "c"),
        check_vma=False,
    )
```

```python
import functools

import jax
import jax.numpy as jnp
from jax import lax
from jax.experimental import pallas as pl
from jax.experimental.pallas import tpu as pltpu
from jax.sharding import Mesh, PartitionSpec as P

PANEL = 256
PANELS = 4
TILE = 32
NPIV = PANEL * PANELS
FRONTS = 32
SLOTS = 32
FRONT_CHILD = 1024
HALF = PANEL // 2
BASE = 8
LEAF = 128

CHIPS = ("z", "y", "h", "l")
NEAR = [[zy * 4 + x for zy in range(16) for x in pair] for pair in ((0, 3), (1, 2))]
SWAP = [(0, 1), (1, 0)]
CHUNKS = ((512, 1536), (2048, 1024), (3072, 512), (3584, 512))
SHARE = 512
ROUNDS = (
    (((0, 1), (0, 2)), ((0, 3), (1, 1))),
    (((1, 2), (1, 3), (3, 3)), ((2, 2), (2, 3), (0, 0))),
)

F32 = jnp.float32
BF16 = jnp.bfloat16
EXACT = lax.Precision.HIGHEST
VMEM_LIMIT = 60 * 1024 * 1024
NN = (((1,), (0,)), ((), ()))
NT = (((1,), (1,)), ((), ()))
TN = (((0,), (0,)), ((), ()))


def cost(micros):
    return pl.CostEstimate(
        flops=int(micros * 1.1e9), bytes_accessed=int(micros * 3.5e6), transcendentals=0
    )


def split_two(value):
    high = value.astype(BF16)
    return high, (value - high.astype(F32)).astype(BF16)


def dot_split(left, right, dims=NN):
    out = lax.dot_general(left[0], right[0], dims, preferred_element_type=F32)
    out += lax.dot_general(left[0], right[1], dims, preferred_element_type=F32)
    return out + lax.dot_general(left[1], right[0], dims, preferred_element_type=F32)


def dot_exact(left, right, dims=NN):
    return lax.dot_general(left, right, dims, precision=EXACT, preferred_element_type=F32)


def pick_kernel(list_ref, pick_ref):
    front = lax.shift_right_logical(list_ref[...], 10)
    rows = front.shape[1]
    hit = lax.broadcasted_iota(jnp.int32, (FRONTS, rows), 0) == front
    order = lax.broadcasted_iota(jnp.int32, (rows, rows), 0) <= lax.broadcasted_iota(
        jnp.int32, (rows, rows), 1
    )
    hit_one = jnp.where(hit, 1.0, 0.0)
    count = jnp.dot(
        hit_one.astype(BF16),
        jnp.where(order, 1.0, 0.0).astype(BF16),
        preferred_element_type=F32,
    )
    rank = jnp.sum(hit_one * count, axis=0, keepdims=True) - 1.0
    slot = front * SLOTS + rank.astype(jnp.int32)
    places = lax.broadcasted_iota(jnp.int32, (FRONTS * SLOTS, rows), 0)
    pick_ref[...] = jnp.where(places == slot, 1.0, 0.0).astype(BF16)


def pick_matrix(list_row):
    rows = list_row.shape[1]
    return pl.pallas_call(
        pick_kernel,
        out_shape=jax.ShapeDtypeStruct((FRONTS * SLOTS, rows), BF16),
        compiler_params=pltpu.CompilerParams(vmem_limit_bytes=VMEM_LIMIT),
        cost_estimate=cost(2),
        name="pick_matrix",
    )(list_row)


def place_rows(pick, value, out_ref):
    high = value.astype(BF16)
    rest = value - high.astype(F32)
    middle = rest.astype(BF16)
    low = (rest - middle.astype(F32)).astype(BF16)
    out = jnp.dot(pick, high, preferred_element_type=F32)
    out += jnp.dot(pick, middle, preferred_element_type=F32)
    out_ref[...] = out + jnp.dot(pick, low, preferred_element_type=F32)


def send_kernel(pick_ref, child_ref, out_ref):
    place_rows(pick_ref[...], child_ref[...], out_ref)


def send_share_kernel(own_ref, pick_ref, child_ref, got_ref, out_ref):
    use_got = jnp.logical_and(pl.program_id(0) < SHARE // got_ref.shape[1], own_ref[0] == 0)
    value = jnp.where(use_got, got_ref[...], child_ref[...])
    place_rows(pick_ref[...], value, out_ref)


def send_rows(pick, child_rows, first, width, use_own=None, got=None):
    rows = child_rows.shape[0]
    block = 256 if width == SHARE else 512
    specs = [
        pl.BlockSpec(pick.shape, lambda i: (0, 0)),
        pl.BlockSpec((rows, block), lambda i: (0, first // block + i)),
    ]
    values = [pick, child_rows]
    if got is not None:
        specs = [pl.BlockSpec(memory_space=pltpu.SMEM)] + specs
        last = SHARE // block - 1
        specs.append(pl.BlockSpec((rows, block), lambda i: (0, jnp.minimum(i, last))))
        values = [use_own] + values + [got]
    return pl.pallas_call(
        send_kernel if got is None else send_share_kernel,
        grid=(width // block,),
        in_specs=specs,
        out_specs=pl.BlockSpec((FRONTS * SLOTS, block), lambda i: (0, i)),
        out_shape=jax.ShapeDtypeStruct((FRONTS * SLOTS, width), F32),
        compiler_params=pltpu.CompilerParams(vmem_limit_bytes=VMEM_LIMIT),
        cost_estimate=cost(3 + width / 256),
        name="send_rows",
    )(*values)


def pivot_kernel(core_ref, own_ref, got_ref, orig_ref, orig_got_ref, keep_ref, high_ref, low_ref):
    step = pl.program_id(0)
    core = core_ref[0]
    child = jnp.where(step // 2 == core, own_ref[...], got_ref[...]).T
    orig = jnp.where(core == 0, orig_ref[...], orig_got_ref[...])
    keep = jnp.where(step == 0, keep_ref[...], 1.0)
    orig = (orig * keep).T
    slots = child.shape[1]
    child_high, child_low = split_two(child)
    orig_high, orig_low = split_two(orig)
    high_ref[:, :slots] = child_high
    low_ref[:, :slots] = child_low
    high_ref[:, slots:] = orig_high
    low_ref[:, slots:] = orig_low


def pivot_columns(core, own, got, orig_rows, orig_got, keep):
    slots, orig = own.shape[0], orig_rows.shape[0]
    rows = slots + orig
    return pl.pallas_call(
        pivot_kernel,
        grid=(PANELS,),
        in_specs=[
            pl.BlockSpec(memory_space=pltpu.SMEM),
            pl.BlockSpec((slots, PANEL), lambda i: (0, i % 2)),
            pl.BlockSpec((slots, PANEL), lambda i: (0, i % 2)),
            pl.BlockSpec((orig, PANEL), lambda i: (0, i)),
            pl.BlockSpec((orig, PANEL), lambda i: (0, i)),
            pl.BlockSpec((orig, 1), lambda i: (0, 0)),
        ],
        out_specs=[pl.BlockSpec((PANEL, rows), lambda i: (i, 0))] * 2,
        out_shape=[jax.ShapeDtypeStruct((NPIV, rows), BF16)] * 2,
        compiler_params=pltpu.CompilerParams(vmem_limit_bytes=VMEM_LIMIT),
        cost_estimate=cost(8),
        name="pivot_columns",
    )(core, own, got, orig_rows, orig_got, keep)


def gram_kernel(left_at, right_at, lh_ref, ll_ref, rh_ref, rl_ref, out_ref):
    out_ref[0] = dot_split((lh_ref[...], ll_ref[...]), (rh_ref[...], rl_ref[...]), NT)


def gram_blocks(left_at, right_at, high, low):
    rows = high.shape[1]
    count = left_at.shape[0]
    left = pl.BlockSpec((PANEL, rows), lambda s, a, b: (a[s], 0))
    right = pl.BlockSpec((PANEL, rows), lambda s, a, b: (b[s], 0))
    return pl.pallas_call(
        gram_kernel,
        grid_spec=pltpu.PrefetchScalarGridSpec(
            num_scalar_prefetch=2,
            grid=(count,),
            in_specs=[left, left, right, right],
            out_specs=pl.BlockSpec((1, PANEL, PANEL), lambda s, a, b: (s, 0, 0)),
        ),
        out_shape=jax.ShapeDtypeStruct((count, PANEL, PANEL), F32),
        compiler_params=pltpu.CompilerParams(vmem_limit_bytes=VMEM_LIMIT),
        cost_estimate=cost(2 + 1.5 * count),
        name="gram_blocks",
    )(left_at, right_at, high, low, high, low)


def split_three(value):
    high = value.astype(BF16).astype(F32)
    rest = value - high
    middle = rest.astype(BF16).astype(F32)
    return high, middle, rest - middle


def factor_leaf(square_ref, inv_ref, cols_ref):
    shape = (BASE, LEAF)
    sub = lax.broadcasted_iota(jnp.int32, shape, 0)
    lane = lax.broadcasted_iota(jnp.int32, shape, 1)
    for step in range(LEAF // BASE):
        top = step * BASE
        below = top + BASE
        rows = square_ref[top:below, :]
        unit = jnp.where(lane == sub + top, 1.0, 0.0)
        tail = unit if step == 0 else inv_ref[top:below, :]
        for j in range(BASE):
            cols_ref[BASE * j : BASE * j + BASE, :] = jnp.broadcast_to(
                rows[:, top + j : top + j + 1], shape
            )
        entry = [
            [
                jnp.broadcast_to(cols_ref[BASE * j + i : BASE * j + i + 1, :], shape)
                for j in range(i + 1)
            ]
            for i in range(BASE)
        ]
        inv_diag = []
        for j in range(BASE):
            inv_diag.append(lax.rsqrt(entry[j][j]))
            for i in range(j + 1, BASE):
                entry[i][j] = entry[i][j] * inv_diag[j]
            for i in range(j + 1, BASE):
                for k in range(j + 1, i + 1):
                    entry[i][k] = entry[i][k] - entry[i][j] * entry[k][j]
        inverse = [[None] * BASE for _ in range(BASE)]
        for i in range(BASE):
            inverse[i][i] = inv_diag[i]
            for j in range(i):
                total = entry[i][j] * inverse[j][j]
                for k in range(j + 1, i):
                    total = total + entry[i][k] * inverse[k][j]
                inverse[i][j] = -(total * inv_diag[i])
        def apply(matrix, lower, values):
            out = [None] * len(values)
            for j in range(BASE):
                first = j if lower else 0
                column = matrix[first][j]
                for i in range(first + 1, BASE):
                    column = jnp.where(sub == i, matrix[i][j], column)
                if first:
                    column = jnp.where(sub < first, 0.0, column)
                for n, rows_n in enumerate(values):
                    term = column * rows_n[j]
                    out[n] = term if out[n] is None else out[n] + term
            return out

        row_all = [
            jnp.broadcast_to(square_ref[top + j : top + j + 1, :], shape) for j in range(BASE)
        ]
        tail_all = [jnp.broadcast_to(tail[j : j + 1, :], shape) for j in range(BASE)]
        (done_tail,) = apply(inverse, True, [tail_all])
        inv_ref[top:below, :] = done_tail
        if below < LEAF:
            product = [[None] * BASE for _ in range(BASE)]
            for i in range(BASE):
                for k in range(i + 1):
                    total = None
                    for j in range(i, BASE):
                        term = inverse[j][i] * inverse[j][k]
                        total = term if total is None else total + term
                    product[i][k] = total
                    product[k][i] = total
            part_rows, part_tail = apply(product, False, [row_all, tail_all])
            rh, rm, rl = split_three(rows)
            ph, pm, pll = split_three(part_rows)
            th, tm, tl = split_three(part_tail)
            left = jnp.concatenate([rh, rh, rm, rh, rl, rm], axis=0).astype(BF16)
            right = jnp.concatenate([ph, pm, ph, pll, ph, pm], axis=0).astype(BF16)
            right_tail = jnp.concatenate([th, tm, th, tl, th, tm], axis=0).astype(BF16)
            change = lax.dot_general(
                left, jnp.concatenate([right, right_tail], axis=1), TN, preferred_element_type=F32
            )
            square_ref[below:, :] = square_ref[below:, :] - change[below:, :LEAF]
            if step == 0:
                later = jnp.where(
                    lax.broadcasted_iota(jnp.int32, (LEAF, LEAF), 0)
                    == lax.broadcasted_iota(jnp.int32, (LEAF, LEAF), 1),
                    1.0,
                    0.0,
                )
                inv_ref[below:, :] = later[below:, :] - change[below:, LEAF:]
            else:
                inv_ref[below:, :] = inv_ref[below:, :] - change[below:, LEAF:]


def gram_block(pair, is_first, own_ref, got_ref):
    for blocks in ROUNDS:
        for core, names in enumerate(blocks):
            if pair in names:
                at = names.index(pair)
                mine = is_first if core == 0 else jnp.logical_not(is_first)
                return jnp.where(mine, own_ref[at], got_ref[at])


def panel_kernel(panel, *refs):
    core_ref, high_ref, low_ref, own_ref, got_ref = refs[:5]
    refs = refs[5:]
    is_first = core_ref[0] == 0
    if panel == 0:
        rows, bases = [], []
        inv_out, diag_out, qh_ref, ql_ref, work, inv_ref, cols_ref = refs
        square = own_ref[...] + got_ref[...]
    else:
        rows = list(refs[: panel - 1])
        refs = refs[panel - 1 :]
        bases = refs[: 2 * panel]
        last_inv, last_diag = refs[2 * panel : 2 * panel + 2]
        inv_out, diag_out, qh_ref, ql_ref, row_out, work, inv_ref, cols_ref = refs[2 * panel + 2 :]
        last = panel - 1
        first = panel * PANEL
        behind = jnp.concatenate(
            [gram_block((last, j), is_first, own_ref, got_ref) for j in range(panel, PANELS)],
            axis=1,
        )
        for old in rows:
            tie = old[:, last * PANEL : first].T
            behind -= dot_exact(tie, old[:, first:])
        if last:
            row_out[:, : last * PANEL] = jnp.zeros((PANEL, last * PANEL), F32)
        row_out[:, last * PANEL : first] = last_diag[...]
        row_out[:, first:] = dot_exact(last_inv[...], behind)
        rows.append(row_out)
        square = gram_block((panel, panel), is_first, own_ref, got_ref)
    pivots = high_ref[...].astype(F32) + low_ref[...].astype(F32)
    for k, old in enumerate(rows):
        tie = old[:, panel * PANEL : (panel + 1) * PANEL].T
        square -= dot_exact(tie, tie, NT)
        pivots -= dot_split(split_two(tie), (bases[2 * k][...], bases[2 * k + 1][...]))
    work[...] = square[:LEAF, :LEAF]
    factor_leaf(work, inv_ref, cols_ref)
    inv_first = inv_ref[...]
    upper = dot_exact(inv_first, square[:LEAF, LEAF:])
    work[...] = square[LEAF:, LEAF:] - dot_exact(upper, upper, TN)
    inv_out[:LEAF, :LEAF] = inv_first
    inv_out[:LEAF, LEAF:] = jnp.zeros((LEAF, LEAF), F32)
    factor_leaf(work, inv_ref, cols_ref)
    inv_second = inv_ref[...]
    inv_out[LEAF:, LEAF:] = inv_second
    inv_out[LEAF:, :LEAF] = -dot_exact(inv_second, dot_exact(upper, inv_first, TN))
    inverse = inv_out[...]
    diag_out[...] = dot_exact(inverse, square)
    qh_ref[...], ql_ref[...] = split_two(dot_split(split_two(inverse), split_two(pivots)))


def factor_panel(panel, core, high, low, own, got, rows, bases, last):
    count = high.shape[1]
    mine = pl.BlockSpec((PANEL, count), lambda i: (panel, 0))
    flat = [*rows, *[value for pair in bases for value in pair], *last]
    full = lambda value: pl.BlockSpec(value.shape, lambda i: (0,) * len(value.shape))
    outs = [jax.ShapeDtypeStruct((PANEL, PANEL), F32)] * 2
    outs += [jax.ShapeDtypeStruct((PANEL, count), BF16)] * 2
    if panel:
        outs.append(jax.ShapeDtypeStruct((PANEL, NPIV), F32))
    return pl.pallas_call(
        functools.partial(panel_kernel, panel),
        grid=(1,),
        in_specs=[pl.BlockSpec(memory_space=pltpu.SMEM), mine, mine, full(own), full(got)]
        + [full(value) for value in flat],
        out_specs=[full(value) for value in outs],
        out_shape=outs,
        scratch_shapes=[pltpu.VMEM((LEAF, LEAF), F32)] * 2 + [pltpu.VMEM((BASE * BASE, LEAF), F32)],
        compiler_params=pltpu.CompilerParams(vmem_limit_bytes=VMEM_LIMIT),
        cost_estimate=cost(15),
        name=f"factor_panel_{panel}",
    )(core, high, low, own, got, *flat)


def project_kernel(count, shared, place_ref, child_ref, orig_ref, *refs):
    if shared:
        other_ref, refs = refs[0], refs[1:]
        use_other = jnp.logical_and(pl.program_id(0) == 0, place_ref[1] == 0)
        orig = jnp.where(use_other, other_ref[...], orig_ref[...])
    else:
        orig = orig_ref[...]
    q_refs, (keep_ref, send_ref, total) = refs[: 2 * count], refs[2 * count :]
    slots = child_ref.shape[0]
    child = split_two(child_ref[...])
    orig = split_two(orig)
    high = jnp.concatenate([ref[...] for ref in q_refs[0::2]], axis=0)
    low = jnp.concatenate([ref[...] for ref in q_refs[1::2]], axis=0)
    total[...] = dot_split((high[:, :slots], low[:, :slots]), child) + dot_split(
        (high[:, slots:], low[:, slots:]), orig
    )
    side = place_ref[0]
    for i in range(count):
        keep_ref[i] = total[pl.ds(i * PANEL + side * HALF, HALF), :]
        send_ref[i] = total[pl.ds(i * PANEL + (1 - side) * HALF, HALF), :]


def project(place, child, orig_rows, first, skip, width, bases, other, hides):
    slots = child.shape[0]
    orig = orig_rows.shape[0]
    count = len(bases)
    block = 512
    flat = [value for pair in bases for value in pair]
    specs = [pl.BlockSpec(value.shape, lambda i: (0, 0)) for value in flat]
    if other is not None:
        flat = [other] + flat
        specs = [pl.BlockSpec((orig, block), lambda i: (0, 0))] + specs
    out = pl.BlockSpec((count, HALF, block), lambda i: (0, 0, i))
    return pl.pallas_call(
        functools.partial(project_kernel, count, other is not None),
        grid=(width // block,),
        in_specs=[
            pl.BlockSpec(memory_space=pltpu.SMEM),
            pl.BlockSpec((slots, block), lambda i: (0, skip // block + i)),
            pl.BlockSpec((orig, block), lambda i: (0, (first + skip) // block + i)),
        ]
        + specs,
        out_specs=[out, out],
        out_shape=[jax.ShapeDtypeStruct((count, HALF, width), F32)] * 2,
        scratch_shapes=[pltpu.VMEM((count * PANEL, block), F32)],
        compiler_params=pltpu.CompilerParams(vmem_limit_bytes=VMEM_LIMIT),
        cost_estimate=cost(15 if hides else 0.5),
        name="project",
    )(place, child, orig_rows, *flat)


def combine_kernel(groups, core_ref, pivot_ref, extra_ref, other_ref, *refs):
    refs, out_ref = refs[:-1], refs[-1]
    panel = pl.program_id(0)
    is_first = core_ref[0] == 0
    out_ref[0, :, :SHARE] = jnp.where(is_first, pivot_ref[0, :, :SHARE], other_ref[0])
    out_ref[0, :, SHARE:NPIV] = jnp.where(is_first, pivot_ref[0, :, SHARE:], extra_ref[0])
    at = 0
    for base, width, skip, first, count in groups:
        mine, got = refs[at : at + 2]
        at += 2

        @pl.when(jnp.logical_and(panel >= first, panel < first + count))
        def _():
            out_ref[0, :, base : base + width] = mine[0, :, skip:] + got[0, :, skip:]


def combine(core, pivot_rows, extra, other, parts, columns):
    groups, values, places = [], [pivot_rows, extra, other], [0, 0, 0]
    base = NPIV
    for pairs in parts:
        first = 0
        for (mine, got), skip in pairs:
            width = mine.shape[2] - skip
            groups.append((base, width, skip, first, mine.shape[0]))
            values += [mine, got]
            places.extend([first, first])
            first += mine.shape[0]
        base += width

    def spec(value, first):
        panels, half, width = value.shape
        return pl.BlockSpec(
            (1, half, width), lambda p: (jnp.clip(p - first, 0, panels - 1), 0, 0)
        )

    return pl.pallas_call(
        functools.partial(combine_kernel, groups),
        grid=(PANELS,),
        in_specs=[pl.BlockSpec(memory_space=pltpu.SMEM)]
        + [spec(value, first) for value, first in zip(values, places)],
        out_specs=pl.BlockSpec((1, HALF, columns), lambda p: (p, 0, 0)),
        out_shape=jax.ShapeDtypeStruct((PANELS, HALF, columns), F32),
        compiler_params=pltpu.CompilerParams(vmem_limit_bytes=VMEM_LIMIT),
        cost_estimate=cost(15),
        name="combine",
    )(core, *values)


def finish_kernel(mine_ref, got_ref, _, out_ref):
    out_ref[...] = mine_ref[...] + got_ref[...]


def finish(mine, got, result):
    panels, half, width = mine.shape
    last = result.shape[2] // width - 1
    part = pl.BlockSpec((panels // 2, half, width), lambda p: (p, 0, 0))
    return pl.pallas_call(
        finish_kernel,
        grid=(2,),
        in_specs=[part, part, pl.BlockSpec(memory_space=pl.ANY)],
        out_specs=pl.BlockSpec((panels // 2, half, width), lambda p: (p, 0, last)),
        out_shape=jax.ShapeDtypeStruct(result.shape, F32),
        input_output_aliases={2: 0},
        compiler_params=pltpu.CompilerParams(vmem_limit_bytes=VMEM_LIMIT),
        cost_estimate=cost(2),
        name="finish",
    )(mine, got, result)


def exchange(sent):
    width = sent.shape[1]
    got = lax.all_to_all(
        sent.reshape(FRONTS, SLOTS, width), CHIPS, 0, 0, axis_index_groups=NEAR, tiled=True
    )
    return got.reshape(FRONTS * SLOTS, width)


def body(child_rows, row_list, orig_rows, tile_mask):
    core = lax.axis_index("c")
    side = lax.axis_index("l")
    core_one = core.astype(jnp.int32).reshape(1)
    place = jnp.stack([side, core]).astype(jnp.int32)

    latest = [None]

    def then(value, *others):
        waits = [other for other in (latest[0], *others) if other is not None]
        return lax.optimization_barrier((value, *waits))[0] if waits else value

    def did(value):
        latest[0] = value
        return value

    def next_chunk(got, sent, *waits):
        got, sent, *_ = lax.optimization_barrier((got, sent, latest[0], *waits))
        latest[0] = got
        return got, exchange(sent)

    give = lax.dynamic_slice_in_dim(child_rows, (1 - core) * SHARE, SHARE, axis=1)
    take = lax.ppermute(give, "c", SWAP)
    pick = did(pick_matrix(row_list.reshape(1, -1)))
    sent_pivot = did(send_rows(then(pick), child_rows, 0, SHARE, 1 - core_one, take))
    got_pivot = exchange(sent_pivot)
    orig_got = lax.ppermute(then(orig_rows)[:, :NPIV], "c", SWAP)
    sents = [did(send_rows(then(pick), child_rows, *CHUNKS[0], core_one, take))]
    sents.append(did(send_rows(then(pick), child_rows, *CHUNKS[1])))
    sents.append(did(send_rows(then(pick), child_rows, *CHUNKS[2])))
    sents.append(did(send_rows(then(pick, orig_got), child_rows, *CHUNKS[3])))
    got_pivot, coming = next_chunk(got_pivot, sents[0])
    pivot_other = lax.ppermute(got_pivot, "c", SWAP)

    keep = jnp.repeat(tile_mask, TILE).astype(F32)[:, None]
    high, low = pivot_columns(core_one, then(got_pivot), pivot_other, orig_rows, orig_got, keep)
    did(high)
    zero = jnp.zeros((1,), jnp.int32)
    corner = did(gram_blocks(zero, zero, then(high), low))
    corner_got = lax.ppermute(corner, "l", SWAP)
    parts, sums = [], []

    def gram_round():
        table = jnp.array(ROUNDS[len(parts)], jnp.int32)[core]
        part = did(gram_blocks(table[:, 0], table[:, 1], then(high), low))
        parts.append((part, lax.ppermute(part, "l", SWAP)))

    def sum_round():
        part, got = parts[len(sums)]
        part = part + then(got)
        sums.append((part, lax.ppermute(part, "c", SWAP)))

    gram_round()
    rows, bases, last = [], [], []

    def panel_step(*waits):
        panel = len(bases)
        own, got = (corner[0], corner_got[0]) if panel == 0 else sums[min(panel - 1, 1)]
        out = factor_panel(panel, core_one, then(high, *waits), low, own, got, rows, bases, last)
        if panel:
            rows.append(out[4])
        bases.append(out[2:4])
        last[:] = out[:2]
        did(out[2])

    def rows_of(panels, child, index, *waits, skip=0, width=SHARE, other=None, hides=False):
        mine, theirs = project(
            place,
            then(child, *waits),
            orig_rows,
            CHUNKS[index][0],
            skip,
            width,
            [bases[p] for p in panels],
            other,
            hides,
        )
        did(theirs)
        return mine, lax.ppermute(theirs, "l", SWAP)

    every = (0, 1, 2, 3)
    panel_step()
    sum_round()
    gram_round()
    panel_step()
    sum_round()
    panel_step()
    here, coming = next_chunk(coming, sents[1])
    early = rows_of((0, 1, 2), here, 0, width=1536, other=orig_got)
    panel_step()
    late = rows_of((3,), here, 0, width=1536, other=orig_got)
    second_here, coming = next_chunk(coming, sents[2])
    second = rows_of(every, second_here, 1, width=1024)
    third_here, coming = next_chunk(coming, sents[3], early[1], late[1])
    third = rows_of(every, third_here, 2)
    mine, got = rows_of(every, coming, 3, second[1])

    extra = jnp.concatenate(
        [own[:, :, :SHARE] + other[:, :, :SHARE] for own, other in (early, late)]
    )
    other_extra = lax.ppermute(extra, "c", [(0, 1)])
    pivot_rows = jnp.stack(rows + [jnp.pad(last[1], ((0, 0), (NPIV - PANEL, 0)))])
    pivot_rows = lax.dynamic_slice_in_dim(pivot_rows, side * HALF, HALF, 1)
    result = combine(
        core_one,
        then(pivot_rows),
        extra,
        other_extra,
        ([(early, SHARE), (late, SHARE)], [(second, 0)], [(third, 0)]),
        child_rows.shape[1],
    )
    return finish(mine, got, result)[None]


def solution(mesh):
    chips = Mesh(mesh.devices.reshape(4, 4, 2, 2, 2), CHIPS + ("c",))
    placed = (P(CHIPS, "c"), P(CHIPS), P(CHIPS, "c"), P(CHIPS))
    return jax.shard_map(
        body,
        mesh=chips,
        in_specs=placed,
        out_specs=P(("z", "y", "h"), None, "l", "c"),
        check_vma=False,
    )
```

```python
import functools

import jax
import jax.numpy as jnp
from jax import lax
from jax.experimental import pallas as pl
from jax.experimental.pallas import tpu as pltpu
from jax.sharding import Mesh, PartitionSpec as P

PANEL = 256
PANELS = 4
TILE = 32
NPIV = PANEL * PANELS
FRONTS = 32
SLOTS = 32
FRONT_CHILD = 1024
HALF = PANEL // 2
BASE = 8
LEAF = 128

CHIPS = ("z", "y", "h", "l")
NEAR = [[zy * 4 + x for zy in range(16) for x in pair] for pair in ((0, 3), (1, 2))]
SWAP = [(0, 1), (1, 0)]
CHUNKS = ((512, 1536), (2048, 1024), (3072, 512), (3584, 512))
SHARE = 512
ROUNDS = (
    (((0, 1), (0, 2)), ((0, 3), (1, 1))),
    (((1, 2), (1, 3), (3, 3)), ((2, 2), (2, 3), (0, 0))),
)

F32 = jnp.float32
BF16 = jnp.bfloat16
EXACT = lax.Precision.HIGHEST
VMEM_LIMIT = 60 * 1024 * 1024
NN = (((1,), (0,)), ((), ()))
NT = (((1,), (1,)), ((), ()))
TN = (((0,), (0,)), ((), ()))


def cost(micros):
    return pl.CostEstimate(
        flops=int(micros * 1.1e9), bytes_accessed=int(micros * 3.5e6), transcendentals=0
    )


def split_two(value):
    high = value.astype(BF16)
    return high, (value - high.astype(F32)).astype(BF16)


def dot_split(left, right, dims=NN):
    out = lax.dot_general(left[0], right[0], dims, preferred_element_type=F32)
    out += lax.dot_general(left[0], right[1], dims, preferred_element_type=F32)
    return out + lax.dot_general(left[1], right[0], dims, preferred_element_type=F32)


def dot_exact(left, right, dims=NN):
    return lax.dot_general(left, right, dims, precision=EXACT, preferred_element_type=F32)


def pick_kernel(list_ref, pick_ref):
    front = lax.shift_right_logical(list_ref[...], 10)
    rows = front.shape[1]
    hit = lax.broadcasted_iota(jnp.int32, (FRONTS, rows), 0) == front
    order = lax.broadcasted_iota(jnp.int32, (rows, rows), 0) <= lax.broadcasted_iota(
        jnp.int32, (rows, rows), 1
    )
    hit_one = jnp.where(hit, 1.0, 0.0)
    count = jnp.dot(
        hit_one.astype(BF16),
        jnp.where(order, 1.0, 0.0).astype(BF16),
        preferred_element_type=F32,
    )
    rank = jnp.sum(hit_one * count, axis=0, keepdims=True) - 1.0
    slot = front * SLOTS + rank.astype(jnp.int32)
    places = lax.broadcasted_iota(jnp.int32, (FRONTS * SLOTS, rows), 0)
    pick_ref[...] = jnp.where(places == slot, 1.0, 0.0).astype(BF16)


def pick_matrix(list_row):
    rows = list_row.shape[1]
    return pl.pallas_call(
        pick_kernel,
        out_shape=jax.ShapeDtypeStruct((FRONTS * SLOTS, rows), BF16),
        compiler_params=pltpu.CompilerParams(vmem_limit_bytes=VMEM_LIMIT),
        cost_estimate=cost(2),
        name="pick_matrix",
    )(list_row)


def place_rows(pick, value, out_ref):
    high = value.astype(BF16)
    rest = value - high.astype(F32)
    middle = rest.astype(BF16)
    low = (rest - middle.astype(F32)).astype(BF16)
    out = jnp.dot(pick, high, preferred_element_type=F32)
    out += jnp.dot(pick, middle, preferred_element_type=F32)
    out_ref[...] = out + jnp.dot(pick, low, preferred_element_type=F32)


def send_kernel(pick_ref, child_ref, out_ref):
    place_rows(pick_ref[...], child_ref[...], out_ref)


def send_share_kernel(own_ref, pick_ref, child_ref, got_ref, out_ref):
    use_got = jnp.logical_and(pl.program_id(0) < SHARE // got_ref.shape[1], own_ref[0] == 0)
    value = jnp.where(use_got, got_ref[...], child_ref[...])
    place_rows(pick_ref[...], value, out_ref)


def send_rows(pick, child_rows, first, width, use_own=None, got=None):
    rows = child_rows.shape[0]
    block = 256 if width == SHARE else 512
    specs = [
        pl.BlockSpec(pick.shape, lambda i: (0, 0)),
        pl.BlockSpec((rows, block), lambda i: (0, first // block + i)),
    ]
    values = [pick, child_rows]
    if got is not None:
        specs = [pl.BlockSpec(memory_space=pltpu.SMEM)] + specs
        last = SHARE // block - 1
        specs.append(pl.BlockSpec((rows, block), lambda i: (0, jnp.minimum(i, last))))
        values = [use_own] + values + [got]
    return pl.pallas_call(
        send_kernel if got is None else send_share_kernel,
        grid=(width // block,),
        in_specs=specs,
        out_specs=pl.BlockSpec((FRONTS * SLOTS, block), lambda i: (0, i)),
        out_shape=jax.ShapeDtypeStruct((FRONTS * SLOTS, width), F32),
        compiler_params=pltpu.CompilerParams(vmem_limit_bytes=VMEM_LIMIT),
        cost_estimate=cost(3 + width / 256),
        name="send_rows",
    )(*values)


def pivot_kernel(core_ref, own_ref, got_ref, orig_ref, orig_got_ref, keep_ref, high_ref, low_ref):
    step = pl.program_id(0)
    core = core_ref[0]
    child = jnp.where(step // 2 == core, own_ref[...], got_ref[...]).T
    orig = jnp.where(core == 0, orig_ref[...], orig_got_ref[...])
    keep = jnp.where(step == 0, keep_ref[...], 1.0)
    orig = (orig * keep).T
    slots = child.shape[1]
    child_high, child_low = split_two(child)
    orig_high, orig_low = split_two(orig)
    high_ref[:, :slots] = child_high
    low_ref[:, :slots] = child_low
    high_ref[:, slots:] = orig_high
    low_ref[:, slots:] = orig_low


def pivot_columns(core, own, got, orig_rows, orig_got, keep):
    slots, orig = own.shape[0], orig_rows.shape[0]
    rows = slots + orig
    return pl.pallas_call(
        pivot_kernel,
        grid=(PANELS,),
        in_specs=[
            pl.BlockSpec(memory_space=pltpu.SMEM),
            pl.BlockSpec((slots, PANEL), lambda i: (0, i % 2)),
            pl.BlockSpec((slots, PANEL), lambda i: (0, i % 2)),
            pl.BlockSpec((orig, PANEL), lambda i: (0, i)),
            pl.BlockSpec((orig, PANEL), lambda i: (0, i)),
            pl.BlockSpec((orig, 1), lambda i: (0, 0)),
        ],
        out_specs=[pl.BlockSpec((PANEL, rows), lambda i: (i, 0))] * 2,
        out_shape=[jax.ShapeDtypeStruct((NPIV, rows), BF16)] * 2,
        compiler_params=pltpu.CompilerParams(vmem_limit_bytes=VMEM_LIMIT),
        cost_estimate=cost(8),
        name="pivot_columns",
    )(core, own, got, orig_rows, orig_got, keep)


def gram_kernel(left_at, right_at, lh_ref, ll_ref, rh_ref, rl_ref, out_ref):
    out_ref[0] = dot_split((lh_ref[...], ll_ref[...]), (rh_ref[...], rl_ref[...]), NT)


def gram_blocks(left_at, right_at, high, low):
    rows = high.shape[1]
    count = left_at.shape[0]
    left = pl.BlockSpec((PANEL, rows), lambda s, a, b: (a[s], 0))
    right = pl.BlockSpec((PANEL, rows), lambda s, a, b: (b[s], 0))
    return pl.pallas_call(
        gram_kernel,
        grid_spec=pltpu.PrefetchScalarGridSpec(
            num_scalar_prefetch=2,
            grid=(count,),
            in_specs=[left, left, right, right],
            out_specs=pl.BlockSpec((1, PANEL, PANEL), lambda s, a, b: (s, 0, 0)),
        ),
        out_shape=jax.ShapeDtypeStruct((count, PANEL, PANEL), F32),
        compiler_params=pltpu.CompilerParams(vmem_limit_bytes=VMEM_LIMIT),
        cost_estimate=cost(2 + 1.5 * count),
        name="gram_blocks",
    )(left_at, right_at, high, low, high, low)


def split_three(value):
    high = value.astype(BF16).astype(F32)
    rest = value - high
    middle = rest.astype(BF16).astype(F32)
    return high, middle, rest - middle


def factor_leaf(square_ref, inv_ref, cols_ref):
    shape = (BASE, LEAF)
    sub = lax.broadcasted_iota(jnp.int32, shape, 0)
    lane = lax.broadcasted_iota(jnp.int32, shape, 1)
    for step in range(LEAF // BASE):
        top = step * BASE
        below = top + BASE
        rows = square_ref[top:below, :]
        unit = jnp.where(lane == sub + top, 1.0, 0.0)
        tail = unit if step == 0 else inv_ref[top:below, :]
        for j in range(BASE):
            cols_ref[BASE * j : BASE * j + BASE, :] = jnp.broadcast_to(
                rows[:, top + j : top + j + 1], shape
            )
        entry = [
            [
                jnp.broadcast_to(cols_ref[BASE * j + i : BASE * j + i + 1, :], shape)
                for j in range(i + 1)
            ]
            for i in range(BASE)
        ]
        inv_diag = []
        for j in range(BASE):
            inv_diag.append(lax.rsqrt(entry[j][j]))
            for i in range(j + 1, BASE):
                entry[i][j] = entry[i][j] * inv_diag[j]
            for i in range(j + 1, BASE):
                for k in range(j + 1, i + 1):
                    entry[i][k] = entry[i][k] - entry[i][j] * entry[k][j]
        inverse = [[None] * BASE for _ in range(BASE)]
        for i in range(BASE):
            inverse[i][i] = inv_diag[i]
            for j in range(i):
                total = entry[i][j] * inverse[j][j]
                for k in range(j + 1, i):
                    total = total + entry[i][k] * inverse[k][j]
                inverse[i][j] = -(total * inv_diag[i])
        def apply(matrix, lower, values):
            out = [None] * len(values)
            for j in range(BASE):
                first = j if lower else 0
                column = matrix[first][j]
                for i in range(first + 1, BASE):
                    column = jnp.where(sub == i, matrix[i][j], column)
                if first:
                    column = jnp.where(sub < first, 0.0, column)
                for n, rows_n in enumerate(values):
                    term = column * rows_n[j]
                    out[n] = term if out[n] is None else out[n] + term
            return out

        row_all = [
            jnp.broadcast_to(square_ref[top + j : top + j + 1, :], shape) for j in range(BASE)
        ]
        tail_all = [jnp.broadcast_to(tail[j : j + 1, :], shape) for j in range(BASE)]
        (done_tail,) = apply(inverse, True, [tail_all])
        inv_ref[top:below, :] = done_tail
        if below < LEAF:
            product = [[None] * BASE for _ in range(BASE)]
            for i in range(BASE):
                for k in range(i + 1):
                    total = None
                    for j in range(i, BASE):
                        term = inverse[j][i] * inverse[j][k]
                        total = term if total is None else total + term
                    product[i][k] = total
                    product[k][i] = total
            part_rows, part_tail = apply(product, False, [row_all, tail_all])
            rh, rm, rl = split_three(rows)
            ph, pm, pll = split_three(part_rows)
            th, tm, tl = split_three(part_tail)
            left = jnp.concatenate([rh, rh, rm, rh, rl, rm], axis=0).astype(BF16)
            right = jnp.concatenate([ph, pm, ph, pll, ph, pm], axis=0).astype(BF16)
            right_tail = jnp.concatenate([th, tm, th, tl, th, tm], axis=0).astype(BF16)
            change = lax.dot_general(
                left, jnp.concatenate([right, right_tail], axis=1), TN, preferred_element_type=F32
            )
            square_ref[below:, :] = square_ref[below:, :] - change[below:, :LEAF]
            if step == 0:
                later = jnp.where(
                    lax.broadcasted_iota(jnp.int32, (LEAF, LEAF), 0)
                    == lax.broadcasted_iota(jnp.int32, (LEAF, LEAF), 1),
                    1.0,
                    0.0,
                )
                inv_ref[below:, :] = later[below:, :] - change[below:, LEAF:]
            else:
                inv_ref[below:, :] = inv_ref[below:, :] - change[below:, LEAF:]


def gram_block(pair, is_first, own_ref, got_ref):
    for blocks in ROUNDS:
        for core, names in enumerate(blocks):
            if pair in names:
                at = names.index(pair)
                mine = is_first if core == 0 else jnp.logical_not(is_first)
                return jnp.where(mine, own_ref[at], got_ref[at])


def panel_kernel(panel, *refs):
    core_ref, high_ref, low_ref, own_ref, got_ref = refs[:5]
    refs = refs[5:]
    is_first = core_ref[0] == 0
    if panel == 0:
        rows, bases = [], []
        inv_out, diag_out, qh_ref, ql_ref, work, inv_ref, cols_ref = refs
        square = own_ref[...] + got_ref[...]
    else:
        rows = list(refs[: panel - 1])
        refs = refs[panel - 1 :]
        bases = refs[: 2 * panel]
        last_inv, last_diag = refs[2 * panel : 2 * panel + 2]
        inv_out, diag_out, qh_ref, ql_ref, row_out, work, inv_ref, cols_ref = refs[2 * panel + 2 :]
        last = panel - 1
        first = panel * PANEL
        behind = jnp.concatenate(
            [gram_block((last, j), is_first, own_ref, got_ref) for j in range(panel, PANELS)],
            axis=1,
        )
        for old in rows:
            tie = old[:, last * PANEL : first].T
            behind -= dot_exact(tie, old[:, first:])
        if last:
            row_out[:, : last * PANEL] = jnp.zeros((PANEL, last * PANEL), F32)
        row_out[:, last * PANEL : first] = last_diag[...]
        row_out[:, first:] = dot_exact(last_inv[...], behind)
        rows.append(row_out)
        square = gram_block((panel, panel), is_first, own_ref, got_ref)
    pivots = high_ref[...].astype(F32) + low_ref[...].astype(F32)
    for k, old in enumerate(rows):
        tie = old[:, panel * PANEL : (panel + 1) * PANEL].T
        square -= dot_exact(tie, tie, NT)
        pivots -= dot_split(split_two(tie), (bases[2 * k][...], bases[2 * k + 1][...]))
    work[...] = square[:LEAF, :LEAF]
    factor_leaf(work, inv_ref, cols_ref)
    inv_first = inv_ref[...]
    upper = dot_exact(inv_first, square[:LEAF, LEAF:])
    work[...] = square[LEAF:, LEAF:] - dot_exact(upper, upper, TN)
    inv_out[:LEAF, :LEAF] = inv_first
    inv_out[:LEAF, LEAF:] = jnp.zeros((LEAF, LEAF), F32)
    factor_leaf(work, inv_ref, cols_ref)
    inv_second = inv_ref[...]
    inv_out[LEAF:, LEAF:] = inv_second
    inv_out[LEAF:, :LEAF] = -dot_exact(inv_second, dot_exact(upper, inv_first, TN))
    inverse = inv_out[...]
    diag_out[...] = dot_exact(inverse, square)
    qh_ref[...], ql_ref[...] = split_two(dot_split(split_two(inverse), split_two(pivots)))


def factor_panel(panel, core, high, low, own, got, rows, bases, last):
    count = high.shape[1]
    mine = pl.BlockSpec((PANEL, count), lambda i: (panel, 0))
    flat = [*rows, *[value for pair in bases for value in pair], *last]
    full = lambda value: pl.BlockSpec(value.shape, lambda i: (0,) * len(value.shape))
    outs = [jax.ShapeDtypeStruct((PANEL, PANEL), F32)] * 2
    outs += [jax.ShapeDtypeStruct((PANEL, count), BF16)] * 2
    if panel:
        outs.append(jax.ShapeDtypeStruct((PANEL, NPIV), F32))
    return pl.pallas_call(
        functools.partial(panel_kernel, panel),
        grid=(1,),
        in_specs=[pl.BlockSpec(memory_space=pltpu.SMEM), mine, mine, full(own), full(got)]
        + [full(value) for value in flat],
        out_specs=[full(value) for value in outs],
        out_shape=outs,
        scratch_shapes=[pltpu.VMEM((LEAF, LEAF), F32)] * 2 + [pltpu.VMEM((BASE * BASE, LEAF), F32)],
        compiler_params=pltpu.CompilerParams(vmem_limit_bytes=VMEM_LIMIT),
        cost_estimate=cost(15),
        name=f"factor_panel_{panel}",
    )(core, high, low, own, got, *flat)


def project_kernel(count, shared, place_ref, child_ref, orig_ref, *refs):
    if shared:
        other_ref, refs = refs[0], refs[1:]
        use_other = jnp.logical_and(pl.program_id(0) == 0, place_ref[1] == 0)
        orig = jnp.where(use_other, other_ref[...], orig_ref[...])
    else:
        orig = orig_ref[...]
    q_refs, (keep_ref, send_ref, total) = refs[: 2 * count], refs[2 * count :]
    slots = child_ref.shape[0]
    child = split_two(child_ref[...])
    orig = split_two(orig)
    high = jnp.concatenate([ref[...] for ref in q_refs[0::2]], axis=0)
    low = jnp.concatenate([ref[...] for ref in q_refs[1::2]], axis=0)
    total[...] = dot_split((high[:, :slots], low[:, :slots]), child) + dot_split(
        (high[:, slots:], low[:, slots:]), orig
    )
    side = place_ref[0]
    for i in range(count):
        keep_ref[i] = total[pl.ds(i * PANEL + side * HALF, HALF), :]
        send_ref[i] = total[pl.ds(i * PANEL + (1 - side) * HALF, HALF), :]


def project(place, child, orig_rows, first, skip, width, bases, other, hides):
    slots = child.shape[0]
    orig = orig_rows.shape[0]
    count = len(bases)
    block = 512
    flat = [value for pair in bases for value in pair]
    specs = [pl.BlockSpec(value.shape, lambda i: (0, 0)) for value in flat]
    if other is not None:
        flat = [other] + flat
        specs = [pl.BlockSpec((orig, block), lambda i: (0, 0))] + specs
    out = pl.BlockSpec((count, HALF, block), lambda i: (0, 0, i))
    return pl.pallas_call(
        functools.partial(project_kernel, count, other is not None),
        grid=(width // block,),
        in_specs=[
            pl.BlockSpec(memory_space=pltpu.SMEM),
            pl.BlockSpec((slots, block), lambda i: (0, skip // block + i)),
            pl.BlockSpec((orig, block), lambda i: (0, (first + skip) // block + i)),
        ]
        + specs,
        out_specs=[out, out],
        out_shape=[jax.ShapeDtypeStruct((count, HALF, width), F32)] * 2,
        scratch_shapes=[pltpu.VMEM((count * PANEL, block), F32)],
        compiler_params=pltpu.CompilerParams(vmem_limit_bytes=VMEM_LIMIT),
        cost_estimate=cost(15 if hides else 0.5),
        name="project",
    )(place, child, orig_rows, *flat)


def combine_kernel(groups, core_ref, pivot_ref, extra_ref, other_ref, *refs):
    refs, out_ref = refs[:-1], refs[-1]
    panel = pl.program_id(0)
    is_first = core_ref[0] == 0
    out_ref[0, :, :SHARE] = jnp.where(is_first, pivot_ref[0, :, :SHARE], other_ref[0])
    out_ref[0, :, SHARE:NPIV] = jnp.where(is_first, pivot_ref[0, :, SHARE:], extra_ref[0])
    at = 0
    for base, width, skip, first, count in groups:
        mine, got = refs[at : at + 2]
        at += 2

        @pl.when(jnp.logical_and(panel >= first, panel < first + count))
        def _():
            out_ref[0, :, base : base + width] = mine[0, :, skip:] + got[0, :, skip:]


def combine(core, pivot_rows, extra, other, parts, columns):
    groups, values, places = [], [pivot_rows, extra, other], [0, 0, 0]
    base = NPIV
    for pairs in parts:
        first = 0
        for (mine, got), skip in pairs:
            width = mine.shape[2] - skip
            groups.append((base, width, skip, first, mine.shape[0]))
            values += [mine, got]
            places.extend([first, first])
            first += mine.shape[0]
        base += width

    def spec(value, first):
        panels, half, width = value.shape
        return pl.BlockSpec(
            (1, half, width), lambda p: (jnp.clip(p - first, 0, panels - 1), 0, 0)
        )

    return pl.pallas_call(
        functools.partial(combine_kernel, groups),
        grid=(PANELS,),
        in_specs=[pl.BlockSpec(memory_space=pltpu.SMEM)]
        + [spec(value, first) for value, first in zip(values, places)],
        out_specs=pl.BlockSpec((1, HALF, columns), lambda p: (p, 0, 0)),
        out_shape=jax.ShapeDtypeStruct((PANELS, HALF, columns), F32),
        compiler_params=pltpu.CompilerParams(vmem_limit_bytes=VMEM_LIMIT),
        cost_estimate=cost(15),
        name="combine",
    )(core, *values)


def finish_kernel(mine_ref, got_ref, _, out_ref):
    out_ref[...] = mine_ref[...] + got_ref[...]


def finish(mine, got, result):
    panels, half, width = mine.shape
    last = result.shape[2] // width - 1
    part = pl.BlockSpec((panels // 2, half, width), lambda p: (p, 0, 0))
    return pl.pallas_call(
        finish_kernel,
        grid=(2,),
        in_specs=[part, part, pl.BlockSpec(memory_space=pl.ANY)],
        out_specs=pl.BlockSpec((panels // 2, half, width), lambda p: (p, 0, last)),
        out_shape=jax.ShapeDtypeStruct(result.shape, F32),
        input_output_aliases={2: 0},
        compiler_params=pltpu.CompilerParams(vmem_limit_bytes=16 * 1024 * 1024),
        cost_estimate=cost(2),
        name="finish",
    )(mine, got, result)


def exchange(sent):
    width = sent.shape[1]
    got = lax.all_to_all(
        sent.reshape(FRONTS, SLOTS, width), CHIPS, 0, 0, axis_index_groups=NEAR, tiled=True
    )
    return got.reshape(FRONTS * SLOTS, width)


def body(child_rows, row_list, orig_rows, tile_mask):
    core = lax.axis_index("c")
    side = lax.axis_index("l")
    core_one = core.astype(jnp.int32).reshape(1)
    place = jnp.stack([side, core]).astype(jnp.int32)

    latest = [None]

    def then(value, *others):
        waits = [other for other in (latest[0], *others) if other is not None]
        return lax.optimization_barrier((value, *waits))[0] if waits else value

    def did(value):
        latest[0] = value
        return value

    def next_chunk(got, sent, *waits):
        got, sent, *_ = lax.optimization_barrier((got, sent, latest[0], *waits))
        latest[0] = got
        return got, exchange(sent)

    give = lax.dynamic_slice_in_dim(child_rows, (1 - core) * SHARE, SHARE, axis=1)
    take = lax.ppermute(give, "c", SWAP)
    pick = did(pick_matrix(row_list.reshape(1, -1)))
    sent_pivot = did(send_rows(then(pick), child_rows, 0, SHARE, 1 - core_one, take))
    got_pivot = exchange(sent_pivot)
    orig_got = lax.ppermute(then(orig_rows)[:, :NPIV], "c", SWAP)
    sents = [did(send_rows(then(pick), child_rows, *CHUNKS[0], core_one, take))]
    sents.append(did(send_rows(then(pick), child_rows, *CHUNKS[1])))
    sents.append(did(send_rows(then(pick), child_rows, *CHUNKS[2])))
    sents.append(did(send_rows(then(pick, orig_got), child_rows, *CHUNKS[3])))
    got_pivot, coming = next_chunk(got_pivot, sents[0])
    pivot_other = lax.ppermute(got_pivot, "c", SWAP)

    keep = jnp.repeat(tile_mask, TILE).astype(F32)[:, None]
    high, low = pivot_columns(core_one, then(got_pivot), pivot_other, orig_rows, orig_got, keep)
    did(high)
    zero = jnp.zeros((1,), jnp.int32)
    corner = did(gram_blocks(zero, zero, then(high), low))
    corner_got = lax.ppermute(corner, "l", SWAP)
    parts, sums = [], []

    def gram_round():
        table = jnp.array(ROUNDS[len(parts)], jnp.int32)[core]
        part = did(gram_blocks(table[:, 0], table[:, 1], then(high), low))
        parts.append((part, lax.ppermute(part, "l", SWAP)))

    def sum_round():
        part, got = parts[len(sums)]
        part = part + then(got)
        sums.append((part, lax.ppermute(part, "c", SWAP)))

    gram_round()
    rows, bases, last = [], [], []

    def panel_step(*waits):
        panel = len(bases)
        own, got = (corner[0], corner_got[0]) if panel == 0 else sums[min(panel - 1, 1)]
        out = factor_panel(panel, core_one, then(high, *waits), low, own, got, rows, bases, last)
        if panel:
            rows.append(out[4])
        bases.append(out[2:4])
        last[:] = out[:2]
        did(out[2])

    def rows_of(panels, child, index, *waits, skip=0, width=SHARE, other=None, hides=False):
        mine, theirs = project(
            place,
            then(child, *waits),
            orig_rows,
            CHUNKS[index][0],
            skip,
            width,
            [bases[p] for p in panels],
            other,
            hides,
        )
        did(theirs)
        return mine, lax.ppermute(theirs, "l", SWAP)

    every = (0, 1, 2, 3)
    panel_step()
    sum_round()
    gram_round()
    panel_step()
    sum_round()
    panel_step()
    here, coming = next_chunk(coming, sents[1])
    early = rows_of((0, 1, 2), here, 0, width=1536, other=orig_got)
    panel_step()
    late = rows_of((3,), here, 0, width=1536, other=orig_got)
    second_here, coming = next_chunk(coming, sents[2])
    second = rows_of(every, second_here, 1, width=1024)
    third_here, coming = next_chunk(coming, sents[3], early[1], late[1])
    third = rows_of(every, third_here, 2)
    mine, got = rows_of(every, coming, 3, second[1])

    extra = jnp.concatenate(
        [own[:, :, :SHARE] + other[:, :, :SHARE] for own, other in (early, late)]
    )
    other_extra = lax.ppermute(extra, "c", [(0, 1)])
    pivot_rows = jnp.stack(rows + [jnp.pad(last[1], ((0, 0), (NPIV - PANEL, 0)))])
    pivot_rows = lax.dynamic_slice_in_dim(pivot_rows, side * HALF, HALF, 1)
    result = combine(
        core_one,
        then(pivot_rows),
        extra,
        other_extra,
        ([(early, SHARE), (late, SHARE)], [(second, 0)], [(third, 0)]),
        child_rows.shape[1],
    )
    return finish(mine, got, result)[None]


def solution(mesh):
    chips = Mesh(mesh.devices.reshape(4, 4, 2, 2, 2), CHIPS + ("c",))
    placed = (P(CHIPS, "c"), P(CHIPS), P(CHIPS, "c"), P(CHIPS))
    return jax.shard_map(
        body,
        mesh=chips,
        in_specs=placed,
        out_specs=P(("z", "y", "h"), None, "l", "c"),
        check_vma=False,
    )
```

```python
import functools

import jax
import jax.numpy as jnp
from jax import lax
from jax.experimental import pallas as pl
from jax.experimental.pallas import tpu as pltpu
from jax.sharding import Mesh, PartitionSpec as P

PANEL = 256
PANELS = 4
TILE = 32
NPIV = PANEL * PANELS
FRONTS = 32
SLOTS = 32
FRONT_CHILD = 1024
HALF = PANEL // 2
BASE = 8
LEAF = 128

CHIPS = ("z", "y", "h", "l")
NEAR = [[zy * 4 + x for zy in range(16) for x in pair] for pair in ((0, 3), (1, 2))]
SWAP = [(0, 1), (1, 0)]
CHUNKS = ((512, 1536), (2048, 1024), (3072, 512), (3584, 512))
SHARE = 512
ROUNDS = (
    (((0, 1), (0, 2)), ((0, 3), (1, 1))),
    (((1, 2), (1, 3), (3, 3)), ((2, 2), (2, 3), (0, 0))),
)

F32 = jnp.float32
BF16 = jnp.bfloat16
EXACT = lax.Precision.HIGHEST
VMEM_LIMIT = 60 * 1024 * 1024
NN = (((1,), (0,)), ((), ()))
NT = (((1,), (1,)), ((), ()))
TN = (((0,), (0,)), ((), ()))


def cost(micros):
    return pl.CostEstimate(
        flops=int(micros * 1.1e9), bytes_accessed=int(micros * 3.5e6), transcendentals=0
    )


def split_two(value):
    high = value.astype(BF16)
    return high, (value - high.astype(F32)).astype(BF16)


def dot_split(left, right, dims=NN):
    out = lax.dot_general(left[0], right[0], dims, preferred_element_type=F32)
    out += lax.dot_general(left[0], right[1], dims, preferred_element_type=F32)
    return out + lax.dot_general(left[1], right[0], dims, preferred_element_type=F32)


def dot_exact(left, right, dims=NN):
    return lax.dot_general(left, right, dims, precision=EXACT, preferred_element_type=F32)


def pick_kernel(list_ref, pick_ref):
    front = lax.shift_right_logical(list_ref[...], 10)
    rows = front.shape[1]
    hit = lax.broadcasted_iota(jnp.int32, (FRONTS, rows), 0) == front
    order = lax.broadcasted_iota(jnp.int32, (rows, rows), 0) <= lax.broadcasted_iota(
        jnp.int32, (rows, rows), 1
    )
    hit_one = jnp.where(hit, 1.0, 0.0)
    count = jnp.dot(
        hit_one.astype(BF16),
        jnp.where(order, 1.0, 0.0).astype(BF16),
        preferred_element_type=F32,
    )
    rank = jnp.sum(hit_one * count, axis=0, keepdims=True) - 1.0
    slot = front * SLOTS + rank.astype(jnp.int32)
    places = lax.broadcasted_iota(jnp.int32, (FRONTS * SLOTS, rows), 0)
    pick_ref[...] = jnp.where(places == slot, 1.0, 0.0).astype(BF16)


def pick_matrix(list_row):
    rows = list_row.shape[1]
    return pl.pallas_call(
        pick_kernel,
        out_shape=jax.ShapeDtypeStruct((FRONTS * SLOTS, rows), BF16),
        compiler_params=pltpu.CompilerParams(vmem_limit_bytes=VMEM_LIMIT),
        cost_estimate=cost(2),
        name="pick_matrix",
    )(list_row)


def place_rows(pick, value, out_ref):
    high, low = split_two(value)
    out = jnp.dot(pick, high, preferred_element_type=F32)
    out_ref[...] = out + jnp.dot(pick, low, preferred_element_type=F32)


def send_kernel(pick_ref, child_ref, out_ref):
    place_rows(pick_ref[...], child_ref[...], out_ref)


def send_share_kernel(own_ref, pick_ref, child_ref, got_ref, out_ref):
    use_got = jnp.logical_and(pl.program_id(0) < SHARE // got_ref.shape[1], own_ref[0] == 0)
    value = jnp.where(use_got, got_ref[...], child_ref[...])
    place_rows(pick_ref[...], value, out_ref)


def send_rows(pick, child_rows, first, width, use_own=None, got=None):
    rows = child_rows.shape[0]
    block = 256 if width == SHARE else 512
    specs = [
        pl.BlockSpec(pick.shape, lambda i: (0, 0)),
        pl.BlockSpec((rows, block), lambda i: (0, first // block + i)),
    ]
    values = [pick, child_rows]
    if got is not None:
        specs = [pl.BlockSpec(memory_space=pltpu.SMEM)] + specs
        last = SHARE // block - 1
        specs.append(pl.BlockSpec((rows, block), lambda i: (0, jnp.minimum(i, last))))
        values = [use_own] + values + [got]
    return pl.pallas_call(
        send_kernel if got is None else send_share_kernel,
        grid=(width // block,),
        in_specs=specs,
        out_specs=pl.BlockSpec((FRONTS * SLOTS, block), lambda i: (0, i)),
        out_shape=jax.ShapeDtypeStruct((FRONTS * SLOTS, width), F32),
        compiler_params=pltpu.CompilerParams(vmem_limit_bytes=16 * 1024 * 1024 if width == SHARE else VMEM_LIMIT),
        cost_estimate=cost(3 + width / 256),
        name="send_rows",
    )(*values)


def pivot_kernel(core_ref, own_ref, got_ref, orig_ref, orig_got_ref, keep_ref, high_ref, low_ref):
    step = pl.program_id(0)
    core = core_ref[0]
    child = jnp.where(step // 2 == core, own_ref[...], got_ref[...]).T
    orig = jnp.where(core == 0, orig_ref[...], orig_got_ref[...])
    keep = jnp.where(step == 0, keep_ref[...], 1.0)
    orig = (orig * keep).T
    slots = child.shape[1]
    child_high, child_low = split_two(child)
    orig_high, orig_low = split_two(orig)
    high_ref[:, :slots] = child_high
    low_ref[:, :slots] = child_low
    high_ref[:, slots:] = orig_high
    low_ref[:, slots:] = orig_low


def pivot_columns(core, own, got, orig_rows, orig_got, keep):
    slots, orig = own.shape[0], orig_rows.shape[0]
    rows = slots + orig
    return pl.pallas_call(
        pivot_kernel,
        grid=(PANELS,),
        in_specs=[
            pl.BlockSpec(memory_space=pltpu.SMEM),
            pl.BlockSpec((slots, PANEL), lambda i: (0, i % 2)),
            pl.BlockSpec((slots, PANEL), lambda i: (0, i % 2)),
            pl.BlockSpec((orig, PANEL), lambda i: (0, i)),
            pl.BlockSpec((orig, PANEL), lambda i: (0, i)),
            pl.BlockSpec((orig, 1), lambda i: (0, 0)),
        ],
        out_specs=[pl.BlockSpec((PANEL, rows), lambda i: (i, 0))] * 2,
        out_shape=[jax.ShapeDtypeStruct((NPIV, rows), BF16)] * 2,
        compiler_params=pltpu.CompilerParams(vmem_limit_bytes=VMEM_LIMIT),
        cost_estimate=cost(8),
        name="pivot_columns",
    )(core, own, got, orig_rows, orig_got, keep)


def gram_kernel(left_at, right_at, lh_ref, ll_ref, rh_ref, rl_ref, out_ref):
    out_ref[0] = dot_split((lh_ref[...], ll_ref[...]), (rh_ref[...], rl_ref[...]), NT)


def gram_blocks(left_at, right_at, high, low):
    rows = high.shape[1]
    count = left_at.shape[0]
    left = pl.BlockSpec((PANEL, rows), lambda s, a, b: (a[s], 0))
    right = pl.BlockSpec((PANEL, rows), lambda s, a, b: (b[s], 0))
    return pl.pallas_call(
        gram_kernel,
        grid_spec=pltpu.PrefetchScalarGridSpec(
            num_scalar_prefetch=2,
            grid=(count,),
            in_specs=[left, left, right, right],
            out_specs=pl.BlockSpec((1, PANEL, PANEL), lambda s, a, b: (s, 0, 0)),
        ),
        out_shape=jax.ShapeDtypeStruct((count, PANEL, PANEL), F32),
        compiler_params=pltpu.CompilerParams(vmem_limit_bytes=VMEM_LIMIT),
        cost_estimate=cost(2 + 1.5 * count),
        name="gram_blocks",
    )(left_at, right_at, high, low, high, low)


def split_three(value):
    high = value.astype(BF16).astype(F32)
    rest = value - high
    middle = rest.astype(BF16).astype(F32)
    return high, middle, rest - middle


def factor_leaf(square_ref, inv_ref, cols_ref):
    shape = (BASE, LEAF)
    sub = lax.broadcasted_iota(jnp.int32, shape, 0)
    lane = lax.broadcasted_iota(jnp.int32, shape, 1)
    for step in range(LEAF // BASE):
        top = step * BASE
        below = top + BASE
        rows = square_ref[top:below, :]
        unit = jnp.where(lane == sub + top, 1.0, 0.0)
        tail = unit if step == 0 else inv_ref[top:below, :]
        for j in range(BASE):
            cols_ref[BASE * j : BASE * j + BASE, :] = jnp.broadcast_to(
                rows[:, top + j : top + j + 1], shape
            )
        entry = [
            [
                jnp.broadcast_to(cols_ref[BASE * j + i : BASE * j + i + 1, :], shape)
                for j in range(i + 1)
            ]
            for i in range(BASE)
        ]
        inv_diag = []
        for j in range(BASE):
            inv_diag.append(lax.rsqrt(entry[j][j]))
            for i in range(j + 1, BASE):
                entry[i][j] = entry[i][j] * inv_diag[j]
            for i in range(j + 1, BASE):
                for k in range(j + 1, i + 1):
                    entry[i][k] = entry[i][k] - entry[i][j] * entry[k][j]
        inverse = [[None] * BASE for _ in range(BASE)]
        for i in range(BASE):
            inverse[i][i] = inv_diag[i]
            for j in range(i):
                total = entry[i][j] * inverse[j][j]
                for k in range(j + 1, i):
                    total = total + entry[i][k] * inverse[k][j]
                inverse[i][j] = -(total * inv_diag[i])
        def apply(matrix, lower, values):
            out = [None] * len(values)
            for j in range(BASE):
                first = j if lower else 0
                column = matrix[first][j]
                for i in range(first + 1, BASE):
                    column = jnp.where(sub == i, matrix[i][j], column)
                if first:
                    column = jnp.where(sub < first, 0.0, column)
                for n, rows_n in enumerate(values):
                    term = column * rows_n[j]
                    out[n] = term if out[n] is None else out[n] + term
            return out

        row_all = [
            jnp.broadcast_to(square_ref[top + j : top + j + 1, :], shape) for j in range(BASE)
        ]
        tail_all = [jnp.broadcast_to(tail[j : j + 1, :], shape) for j in range(BASE)]
        (done_tail,) = apply(inverse, True, [tail_all])
        inv_ref[top:below, :] = done_tail
        if below < LEAF:
            product = [[None] * BASE for _ in range(BASE)]
            for i in range(BASE):
                for k in range(i + 1):
                    total = None
                    for j in range(i, BASE):
                        term = inverse[j][i] * inverse[j][k]
                        total = term if total is None else total + term
                    product[i][k] = total
                    product[k][i] = total
            part_rows, part_tail = apply(product, False, [row_all, tail_all])
            rh, rm, rl = split_three(rows)
            ph, pm, pll = split_three(part_rows)
            th, tm, tl = split_three(part_tail)
            left = jnp.concatenate([rh, rh, rm, rh, rl, rm], axis=0).astype(BF16)
            right = jnp.concatenate([ph, pm, ph, pll, ph, pm], axis=0).astype(BF16)
            right_tail = jnp.concatenate([th, tm, th, tl, th, tm], axis=0).astype(BF16)
            change = lax.dot_general(
                left, jnp.concatenate([right, right_tail], axis=1), TN, preferred_element_type=F32
            )
            square_ref[below:, :] = square_ref[below:, :] - change[below:, :LEAF]
            if step == 0:
                later = jnp.where(
                    lax.broadcasted_iota(jnp.int32, (LEAF, LEAF), 0)
                    == lax.broadcasted_iota(jnp.int32, (LEAF, LEAF), 1),
                    1.0,
                    0.0,
                )
                inv_ref[below:, :] = later[below:, :] - change[below:, LEAF:]
            else:
                inv_ref[below:, :] = inv_ref[below:, :] - change[below:, LEAF:]


def gram_block(pair, is_first, own_ref, got_ref):
    for blocks in ROUNDS:
        for core, names in enumerate(blocks):
            if pair in names:
                at = names.index(pair)
                mine = is_first if core == 0 else jnp.logical_not(is_first)
                return jnp.where(mine, own_ref[at], got_ref[at])


def panel_kernel(panel, *refs):
    core_ref, high_ref, low_ref, own_ref, got_ref = refs[:5]
    refs = refs[5:]
    is_first = core_ref[0] == 0
    if panel == 0:
        rows, bases = [], []
        inv_out, diag_out, qh_ref, ql_ref, work, inv_ref, cols_ref = refs
        square = own_ref[...] + got_ref[...]
    else:
        rows = list(refs[: panel - 1])
        refs = refs[panel - 1 :]
        bases = refs[: 2 * panel]
        last_inv, last_diag = refs[2 * panel : 2 * panel + 2]
        inv_out, diag_out, qh_ref, ql_ref, row_out, work, inv_ref, cols_ref = refs[2 * panel + 2 :]
        last = panel - 1
        first = panel * PANEL
        behind = jnp.concatenate(
            [gram_block((last, j), is_first, own_ref, got_ref) for j in range(panel, PANELS)],
            axis=1,
        )
        for old in rows:
            tie = old[:, last * PANEL : first].T
            behind -= dot_exact(tie, old[:, first:])
        if last:
            row_out[:, : last * PANEL] = jnp.zeros((PANEL, last * PANEL), F32)
        row_out[:, last * PANEL : first] = last_diag[...]
        row_out[:, first:] = dot_exact(last_inv[...], behind)
        rows.append(row_out)
        square = gram_block((panel, panel), is_first, own_ref, got_ref)
    pivots = high_ref[...].astype(F32) + low_ref[...].astype(F32)
    for k, old in enumerate(rows):
        tie = old[:, panel * PANEL : (panel + 1) * PANEL].T
        square -= dot_exact(tie, tie, NT)
        pivots -= dot_split(split_two(tie), (bases[2 * k][...], bases[2 * k + 1][...]))
    work[...] = square[:LEAF, :LEAF]
    factor_leaf(work, inv_ref, cols_ref)
    inv_first = inv_ref[...]
    upper = dot_exact(inv_first, square[:LEAF, LEAF:])
    work[...] = square[LEAF:, LEAF:] - dot_exact(upper, upper, TN)
    inv_out[:LEAF, :LEAF] = inv_first
    inv_out[:LEAF, LEAF:] = jnp.zeros((LEAF, LEAF), F32)
    factor_leaf(work, inv_ref, cols_ref)
    inv_second = inv_ref[...]
    inv_out[LEAF:, LEAF:] = inv_second
    inv_out[LEAF:, :LEAF] = -dot_exact(inv_second, dot_exact(upper, inv_first, TN))
    inverse = inv_out[...]
    diag_out[...] = dot_exact(inverse, square)
    qh_ref[...], ql_ref[...] = split_two(dot_split(split_two(inverse), split_two(pivots)))


def factor_panel(panel, core, high, low, own, got, rows, bases, last):
    count = high.shape[1]
    mine = pl.BlockSpec((PANEL, count), lambda i: (panel, 0))
    flat = [*rows, *[value for pair in bases for value in pair], *last]
    full = lambda value: pl.BlockSpec(value.shape, lambda i: (0,) * len(value.shape))
    outs = [jax.ShapeDtypeStruct((PANEL, PANEL), F32)] * 2
    outs += [jax.ShapeDtypeStruct((PANEL, count), BF16)] * 2
    if panel:
        outs.append(jax.ShapeDtypeStruct((PANEL, NPIV), F32))
    return pl.pallas_call(
        functools.partial(panel_kernel, panel),
        grid=(1,),
        in_specs=[pl.BlockSpec(memory_space=pltpu.SMEM), mine, mine, full(own), full(got)]
        + [full(value) for value in flat],
        out_specs=[full(value) for value in outs],
        out_shape=outs,
        scratch_shapes=[pltpu.VMEM((LEAF, LEAF), F32)] * 2 + [pltpu.VMEM((BASE * BASE, LEAF), F32)],
        compiler_params=pltpu.CompilerParams(vmem_limit_bytes=VMEM_LIMIT),
        cost_estimate=cost(15),
        name=f"factor_panel_{panel}",
    )(core, high, low, own, got, *flat)


def project_kernel(count, shared, place_ref, child_ref, orig_ref, *refs):
    if shared:
        other_ref, refs = refs[0], refs[1:]
        use_other = jnp.logical_and(pl.program_id(0) == 0, place_ref[1] == 0)
        orig = jnp.where(use_other, other_ref[...], orig_ref[...])
    else:
        orig = orig_ref[...]
    q_refs, (keep_ref, send_ref, total) = refs[: 2 * count], refs[2 * count :]
    slots = child_ref.shape[0]
    child = split_two(child_ref[...])
    orig = split_two(orig)
    high = jnp.concatenate([ref[...] for ref in q_refs[0::2]], axis=0)
    low = jnp.concatenate([ref[...] for ref in q_refs[1::2]], axis=0)
    total[...] = dot_split((high[:, :slots], low[:, :slots]), child) + dot_split(
        (high[:, slots:], low[:, slots:]), orig
    )
    side = place_ref[0]
    for i in range(count):
        keep_ref[i] = total[pl.ds(i * PANEL + side * HALF, HALF), :]
        send_ref[i] = total[pl.ds(i * PANEL + (1 - side) * HALF, HALF), :]


def project(place, child, orig_rows, first, skip, width, bases, other, hides):
    slots = child.shape[0]
    orig = orig_rows.shape[0]
    count = len(bases)
    block = 512
    flat = [value for pair in bases for value in pair]
    specs = [pl.BlockSpec(value.shape, lambda i: (0, 0)) for value in flat]
    if other is not None:
        flat = [other] + flat
        specs = [pl.BlockSpec((orig, block), lambda i: (0, 0))] + specs
    out = pl.BlockSpec((count, HALF, block), lambda i: (0, 0, i))
    return pl.pallas_call(
        functools.partial(project_kernel, count, other is not None),
        grid=(width // block,),
        in_specs=[
            pl.BlockSpec(memory_space=pltpu.SMEM),
            pl.BlockSpec((slots, block), lambda i: (0, skip // block + i)),
            pl.BlockSpec((orig, block), lambda i: (0, (first + skip) // block + i)),
        ]
        + specs,
        out_specs=[out, out],
        out_shape=[jax.ShapeDtypeStruct((count, HALF, width), F32)] * 2,
        scratch_shapes=[pltpu.VMEM((count * PANEL, block), F32)],
        compiler_params=pltpu.CompilerParams(vmem_limit_bytes=VMEM_LIMIT),
        cost_estimate=cost(15 if hides else 0.5),
        name="project",
    )(place, child, orig_rows, *flat)


def combine_kernel(groups, core_ref, pivot_ref, extra_ref, other_ref, *refs):
    refs, out_ref = refs[:-1], refs[-1]
    panel = pl.program_id(0)
    is_first = core_ref[0] == 0
    out_ref[0, :, :SHARE] = jnp.where(is_first, pivot_ref[0, :, :SHARE], other_ref[0])
    out_ref[0, :, SHARE:NPIV] = jnp.where(is_first, pivot_ref[0, :, SHARE:], extra_ref[0])
    at = 0
    for base, width, skip, first, count in groups:
        mine, got = refs[at : at + 2]
        at += 2

        @pl.when(jnp.logical_and(panel >= first, panel < first + count))
        def _():
            out_ref[0, :, base : base + width] = mine[0, :, skip:] + got[0, :, skip:]


def combine(core, pivot_rows, extra, other, parts, columns):
    groups, values, places = [], [pivot_rows, extra, other], [0, 0, 0]
    base = NPIV
    for pairs in parts:
        first = 0
        for (mine, got), skip in pairs:
            width = mine.shape[2] - skip
            groups.append((base, width, skip, first, mine.shape[0]))
            values += [mine, got]
            places.extend([first, first])
            first += mine.shape[0]
        base += width

    def spec(value, first):
        panels, half, width = value.shape
        return pl.BlockSpec(
            (1, half, width), lambda p: (jnp.clip(p - first, 0, panels - 1), 0, 0)
        )

    return pl.pallas_call(
        functools.partial(combine_kernel, groups),
        grid=(PANELS,),
        in_specs=[pl.BlockSpec(memory_space=pltpu.SMEM)]
        + [spec(value, first) for value, first in zip(values, places)],
        out_specs=pl.BlockSpec((1, HALF, columns), lambda p: (p, 0, 0)),
        out_shape=jax.ShapeDtypeStruct((PANELS, HALF, columns), F32),
        compiler_params=pltpu.CompilerParams(vmem_limit_bytes=VMEM_LIMIT),
        cost_estimate=cost(15),
        name="combine",
    )(core, *values)


def finish_kernel(mine_ref, got_ref, _, out_ref):
    out_ref[...] = mine_ref[...] + got_ref[...]


def finish(mine, got, result):
    panels, half, width = mine.shape
    last = result.shape[2] // width - 1
    part = pl.BlockSpec((panels // 2, half, width), lambda p: (p, 0, 0))
    return pl.pallas_call(
        finish_kernel,
        grid=(2,),
        in_specs=[part, part, pl.BlockSpec(memory_space=pl.ANY)],
        out_specs=pl.BlockSpec((panels // 2, half, width), lambda p: (p, 0, last)),
        out_shape=jax.ShapeDtypeStruct(result.shape, F32),
        input_output_aliases={2: 0},
        compiler_params=pltpu.CompilerParams(vmem_limit_bytes=16 * 1024 * 1024),
        cost_estimate=cost(2),
        name="finish",
    )(mine, got, result)


def exchange(sent):
    width = sent.shape[1]
    got = lax.all_to_all(
        sent.reshape(FRONTS, SLOTS, width), CHIPS, 0, 0, axis_index_groups=NEAR, tiled=True
    )
    return got.reshape(FRONTS * SLOTS, width)


def body(child_rows, row_list, orig_rows, tile_mask):
    core = lax.axis_index("c")
    side = lax.axis_index("l")
    core_one = core.astype(jnp.int32).reshape(1)
    place = jnp.stack([side, core]).astype(jnp.int32)

    latest = [None]

    def then(value, *others):
        waits = [other for other in (latest[0], *others) if other is not None]
        return lax.optimization_barrier((value, *waits))[0] if waits else value

    def did(value):
        latest[0] = value
        return value

    def next_chunk(got, sent, *waits):
        got, sent, *_ = lax.optimization_barrier((got, sent, latest[0], *waits))
        latest[0] = got
        return got, exchange(sent)

    give = lax.dynamic_slice_in_dim(child_rows, (1 - core) * SHARE, SHARE, axis=1)
    take = lax.ppermute(give, "c", SWAP)
    pick = did(pick_matrix(row_list.reshape(1, -1)))
    sent_pivot = did(send_rows(then(pick), child_rows, 0, SHARE, 1 - core_one, take))
    got_pivot = exchange(sent_pivot)
    orig_got = lax.ppermute(then(orig_rows)[:, :NPIV], "c", SWAP)
    sents = [did(send_rows(then(pick), child_rows, *CHUNKS[0], core_one, take))]
    sents.append(did(send_rows(then(pick), child_rows, *CHUNKS[1])))
    sents.append(did(send_rows(then(pick), child_rows, *CHUNKS[2])))
    sents.append(did(send_rows(then(pick, orig_got), child_rows, *CHUNKS[3])))
    got_pivot, coming = next_chunk(got_pivot, sents[0])
    pivot_other = lax.ppermute(got_pivot, "c", SWAP)

    keep = jnp.repeat(tile_mask, TILE).astype(F32)[:, None]
    high, low = pivot_columns(core_one, then(got_pivot), pivot_other, orig_rows, orig_got, keep)
    did(high)
    zero = jnp.zeros((1,), jnp.int32)
    corner = did(gram_blocks(zero, zero, then(high), low))
    corner_got = lax.ppermute(corner, "l", SWAP)
    parts, sums = [], []

    def gram_round():
        table = jnp.array(ROUNDS[len(parts)], jnp.int32)[core]
        part = did(gram_blocks(table[:, 0], table[:, 1], then(high), low))
        parts.append((part, lax.ppermute(part, "l", SWAP)))

    def sum_round():
        part, got = parts[len(sums)]
        part = part + then(got)
        sums.append((part, lax.ppermute(part, "c", SWAP)))

    gram_round()
    rows, bases, last = [], [], []

    def panel_step(*waits):
        panel = len(bases)
        own, got = (corner[0], corner_got[0]) if panel == 0 else sums[min(panel - 1, 1)]
        out = factor_panel(panel, core_one, then(high, *waits), low, own, got, rows, bases, last)
        if panel:
            rows.append(out[4])
        bases.append(out[2:4])
        last[:] = out[:2]
        did(out[2])

    def rows_of(panels, child, index, *waits, skip=0, width=SHARE, other=None, hides=False):
        mine, theirs = project(
            place,
            then(child, *waits),
            orig_rows,
            CHUNKS[index][0],
            skip,
            width,
            [bases[p] for p in panels],
            other,
            hides,
        )
        did(theirs)
        return mine, lax.ppermute(theirs, "l", SWAP)

    every = (0, 1, 2, 3)
    panel_step()
    sum_round()
    gram_round()
    panel_step()
    sum_round()
    panel_step()
    here, coming = next_chunk(coming, sents[1])
    early = rows_of((0, 1, 2), here, 0, width=1536, other=orig_got)
    panel_step()
    late = rows_of((3,), here, 0, width=1536, other=orig_got)
    second_here, coming = next_chunk(coming, sents[2])
    second = rows_of(every, second_here, 1, width=1024)
    third_here, coming = next_chunk(coming, sents[3], early[1], late[1])
    third = rows_of(every, third_here, 2)
    mine, got = rows_of(every, coming, 3, second[1])

    extra = jnp.concatenate(
        [own[:, :, :SHARE] + other[:, :, :SHARE] for own, other in (early, late)]
    )
    other_extra = lax.ppermute(extra, "c", [(0, 1)])
    pivot_rows = jnp.stack(rows + [jnp.pad(last[1], ((0, 0), (NPIV - PANEL, 0)))])
    pivot_rows = lax.dynamic_slice_in_dim(pivot_rows, side * HALF, HALF, 1)
    result = combine(
        core_one,
        then(pivot_rows),
        extra,
        other_extra,
        ([(early, SHARE), (late, SHARE)], [(second, 0)], [(third, 0)]),
        child_rows.shape[1],
    )
    return finish(mine, got, result)[None]


def solution(mesh):
    chips = Mesh(mesh.devices.reshape(4, 4, 2, 2, 2), CHIPS + ("c",))
    placed = (P(CHIPS, "c"), P(CHIPS), P(CHIPS, "c"), P(CHIPS))
    return jax.shard_map(
        body,
        mesh=chips,
        in_specs=placed,
        out_specs=P(("z", "y", "h"), None, "l", "c"),
        check_vma=False,
    )
```
